32 devices in a mesh: member: 2 (over y), lon: 16 (over z, x, core).
Axes of the slice: x: 2, y: 2, z: 4, core: 2. Of those that a mesh axis runs over, the one named last changes fastest.
Arguments:
- state_start: float32 [190, 256, 128], P('member', 'lon'), parts along dimension 0, may hold values from -6 to 6
- lift_weight: bfloat16 [95, 256], replicated, may hold values from -0.625 to 0.625
- conv_kernel: float32 [49, 256], replicated, may hold values from -0.875 to 0.875
- norm_gain: float32 [256], replicated, may hold values from 0.1 to 1.9
- up_weight: bfloat16 [256, 1024], replicated, may hold values from -0.375 to 0.375
- down_weight: bfloat16 [1024, 256], replicated, may hold values from -0.1875 to 0.1875
- out_weight: bfloat16 [256, 95], replicated, may hold values from -0.375 to 0.375
- obs_cells: int32 [4, 256, 32, 4], P('member', 'lon'), parts along dimension 0, may hold values from 0 to 127
- obs_weights: float32 [4, 256, 32, 4], P('member', 'lon'), parts along dimension 0, may hold values from 0.1 to 1
- tile_counts: int32 [4, 256], P('member', 'lon'), parts along dimension 0, may hold values from 1 to 32, as said below
- obs_owner: int32 [4, 8192, 1], P('member', 'lon'), parts along dimension 0, may hold values from 0 to 15; in each aligned block of 512 rows (0 to 511, 512 to 1023, ..., all dimensions but the last counted through in order) at most 64 rows name the same one
- obs_values: float32 [4, 16, 16, 64, 95], P('member', 'lon'), parts along dimension 0, may hold values from -6 to 6
- obs_precision: float32 [4, 16, 16, 64, 95], P('member', 'lon'), parts along dimension 0, may hold values from 0.5 to 2
Outputs:
- gradient: float32 [190, 256, 128], P('member', 'lon'), parts along dimension 0
The draws below stay inside these ranges and needn't reach their ends.
There are 2 independent parts, one for each index of `member`. The reference program is written for one: setup_inputs(seed, part) draws one part's arguments, and reference() takes and returns one part's arrays. A program takes and returns all parts, laid end to end along the dimension named above; an argument that names none is the same for every part. Nothing has to cross between parts.
Inputs may be any that keep to these rules, and one draw needn't show every extreme that they name: Slots k >= tile_counts of a tile are padding; some tile of every time holds 32 observations. `obs_owner`: within the 512 slots of one band at one time, no owner is named by more than 64 slots, and some band names one owner exactly 64 times.
All inputs are finite; a program needn't handle non-finite values.
Results may differ from the reference program's by a relative error of at most 0.015.
Values may be sent and summed in bfloat16 or wider, within the bound.
A program may use at most 128 MiB of HBM per device.

```python
import math
import jax
import jax.numpy as jnp
import numpy as np
from jax import lax

S = 95
C = 256
E = 1024
K = 32
P_SIZE = 4
TILE_CELLS = 128
LON_DEV = 16
LAT = 128
LON = 256
TILE_LAT = 8
TILES = 16
TILES_ALL = 256
CAP = 64
N_LON = 16


def draw_tile_counts(key, part):
    key_base, key_level, key_pick = jax.random.split(jax.random.fold_in(key, 17), 3)
    base_counts = jax.random.randint(key_base, (2, TILES_ALL), 1, K + 1)
    band_level = jax.random.randint(key_level, (2, TILES_ALL // TILES, 1), 1, 5)
    band_level = jnp.broadcast_to(band_level, (2, TILES_ALL // TILES, TILES)).reshape(2, TILES_ALL)
    counts = 1 + (base_counts - 1) * band_level // 4
    picked = jax.random.randint(key_pick, (2, 1), 0, TILES_ALL)
    spots = jnp.arange(TILES_ALL, dtype=jnp.int32)[None, :]
    return jnp.where(spots == picked, K, counts).astype(jnp.int32)


def place_ends(values, rng, low, high):
    shape = values.shape
    spot = [jax.random.randint(jax.random.fold_in(rng, axis), (), 0, shape[axis]) for axis in range(len(shape))]
    values = values.at[tuple(spot)].set(low)
    longest = shape.index(max(shape))
    spot[longest] = (spot[longest] + 1) % shape[longest]
    return values.at[tuple(spot)].set(high)


def steps_of(key, extent, cuts, low, top_value):
    level = 1.0
    for axis_at, blocks in cuts:
        heights = jax.random.uniform(jax.random.fold_in(jax.random.fold_in(key, 6), axis_at), (blocks,), jnp.float32, low / len(cuts), top_value / len(cuts))
        level = level * jnp.repeat(jnp.exp(heights), extent[axis_at] // blocks).reshape((-1,) + (1,) * (len(extent) - 1 - axis_at))
    return level


def shared_out(key, own, number, rows, amount, top, limit, lean):
    sequence = jax.random.permutation(key, amount)
    packed, common = portions_of(amount, rows * top, limit, lean, True), portions_of(amount, rows * top, limit, lean, False)
    places = jnp.arange(amount)

    def named(lengths, turn):
        used = int((lengths > 0).sum())
        fixed = max(1, used // 4)
        moved = fixed + (places - fixed + turn * (used - fixed)) % max(1, amount - fixed)
        return jnp.zeros((amount,), jnp.int32).at[sequence[jnp.where(places < fixed, places, moved)]].set(jnp.asarray(lengths, jnp.int32))

    lengths = jnp.where(number % 4 == 0, named(packed, number // 4), named(common, number - number // 4 - 1))
    mixed = jax.random.permutation(jax.random.fold_in(own, 3), amount)
    giver, sink = mixed[0:amount // 2 * 2:2], mixed[1:amount // 2 * 2:2]
    room = jnp.minimum(lengths[giver] - 1, limit - lengths[sink]) // 2
    room = jnp.where((giver == sequence[0]) | (sink == sequence[0]) | (lengths[sink] == 0), 0, jnp.maximum(room, 0))
    moved = jax.random.randint(jax.random.fold_in(own, 4), (amount // 2,), 0, 1 << 20) % (room + 1)
    lengths = lengths.at[giver].add(-moved).at[sink].add(moved)
    members = jnp.searchsorted(jnp.cumsum(lengths), jnp.arange(rows * top), side="right").astype(jnp.int32)
    grid = members.reshape(top, rows).T
    grid = grid[jax.random.permutation(jax.random.fold_in(own, 1), rows)]
    turn = jax.random.randint(jax.random.fold_in(own, 2), (rows, 1), 0, top)
    return jnp.take_along_axis(grid, (jnp.arange(top)[None, :] + turn) % top, axis=1)


def portions_of(number_of, total, reach, skew, full):
    loads = [(1 << 20) // math.isqrt(rank ** skew) + 1 for rank in range(1, number_of + 1)]
    largest = reach if full else min(reach, max(-(-total // number_of), total * loads[0] // sum(loads)))
    least = 1 if total - largest >= number_of - 1 else 0
    given, spare = [largest] + [least] * (number_of - 1), total - largest - least * (number_of - 1)
    while spare > 0:
        candidates = [i for i in range(1, number_of) if given[i] < largest] or [i for i in range(1, number_of) if given[i] < reach]
        pool, left = sum([loads[i] for i in candidates]), spare
        for i in candidates:
            addition = min(reach - given[i], max(1, left * loads[i] // pool), spare)
            given[i] = given[i] + addition
            spare = spare - addition
    return np.array(given)


def normal_values(own_key, shape, scale, bound, cuts=(), held_as=jnp.bfloat16):
    entries = scale * jax.random.normal(own_key, shape, jnp.float32)
    if cuts:
        entries = entries * steps_of(own_key, shape, cuts, -0.22, 0.18)
    return jnp.clip(entries, -bound, bound).astype(held_as)


def setup_inputs(seed: int = 0, part: int = 0) -> dict:
    seeds = jax.random.split(jax.random.key(seed), 14)
    part_splits = jax.random.split(jax.random.fold_in(seeds[13], part), 14)
    state_start = normal_values(part_splits[0], (S, LON, LAT), 1.0, 6.0, ((1, 16),), jnp.float32)
    lift_weight = normal_values(seeds[1], (S, C), S ** -0.5, 0.625)
    conv_kernel = normal_values(seeds[2], (49, C), 49 ** -0.5, 0.875, (), jnp.float32)
    norm_gain = jnp.clip(1.0 + 0.18 * jax.random.normal(seeds[3], (C,), jnp.float32), 0.1, 1.9)
    up_weight = normal_values(seeds[4], (C, E), C ** -0.5, 0.375)
    down_weight = normal_values(seeds[5], (E, C), E ** -0.5, 0.1875)
    out_weight = normal_values(seeds[6], (C, S), C ** -0.5, 0.375)
    obs_cells = place_ends(jax.random.randint(part_splits[7], (2, TILES_ALL, K, P_SIZE), 0, TILE_CELLS), jax.random.fold_in(part_splits[7], 1), 0, TILE_CELLS - 1).astype(jnp.int32)
    obs_weights = jnp.clip(jnp.exp(math.log(1.0) - 2.3025851 * jax.random.uniform(part_splits[8], (2, TILES_ALL, K, P_SIZE), jnp.float32) ** steps_of(part_splits[8], (2, TILES_ALL, K, P_SIZE), ((1, 16),), -0.2, 0.2)), 0.1, 1.0)
    tile_counts = draw_tile_counts(jax.random.fold_in(jax.random.fold_in(seeds[13], part), 71), part)
    obs_owner_keys = jax.random.split(jax.random.fold_in(part_splits[10], 1), 2 * (TILES_ALL * K) // (TILES * K))
    obs_owner_turns = jax.random.permutation(jax.random.fold_in(part_splits[10], 3), 2 * (TILES_ALL * K) // (TILES * K))
    obs_owner = jax.vmap(lambda own, number: shared_out(jax.random.fold_in(part_splits[10], 2), own, number, TILES * K, N_LON, 1, CAP, 2))(obs_owner_keys, obs_owner_turns).reshape((2, TILES_ALL * K, 1))
    obs_values = normal_values(part_splits[11], (2, N_LON, N_LON, CAP, S), 1.0, 6.0, ((1, 16),), jnp.float32)
    obs_precision = jnp.clip(jnp.exp(math.log(2.0) - 1.3862944 * jax.random.uniform(part_splits[12], (2, N_LON, N_LON, CAP, S), jnp.float32) ** steps_of(part_splits[12], (2, N_LON, N_LON, CAP, S), ((1, 16),), -0.2, 0.2)), 0.5, 2.0)
    return {"state_start": state_start, "lift_weight": lift_weight, "conv_kernel": conv_kernel, "norm_gain": norm_gain, "up_weight": up_weight, "down_weight": down_weight, "out_weight": out_weight, "obs_cells": obs_cells, "obs_weights": obs_weights, "tile_counts": tile_counts, "obs_owner": obs_owner, "obs_values": obs_values, "obs_precision": obs_precision}


gelu_coef = 0.044715
root_two_pi = 0.7978845608028654
eps_norm = 1e-06
highest = lax.Precision.HIGHEST

def half_dot(left, right):
    return jnp.dot(left.astype(jnp.float32), right.astype(jnp.float32), precision=highest)

def gelu_value(z):
    inner_arg = root_two_pi * (z + gelu_coef * z * z * z)
    return 0.5 * z * (1.0 + jnp.tanh(inner_arg))

def gelu_slope(z):
    inner_arg = root_two_pi * (z + gelu_coef * z * z * z)
    tanh_val = jnp.tanh(inner_arg)
    return 0.5 * (1.0 + tanh_val) + 0.5 * z * (1.0 - tanh_val * tanh_val) * root_two_pi * (1.0 + 3.0 * gelu_coef * z * z)

def wrap_pad(grid_field, margin):
    wrapped = jnp.concatenate([grid_field[-margin:], grid_field, grid_field[:margin]], axis=0)
    return jnp.pad(wrapped, ((0, 0), (margin, margin), (0, 0)))

def conv_taps(padded, kernel, lon_rows, lat_cols):
    summed = jnp.zeros((lon_rows, lat_cols, padded.shape[2]), jnp.float32)
    for i in range(7):
        for j in range(7):
            summed = summed + kernel[i * 7 + j] * padded[i:i + lon_rows, j:j + lat_cols].astype(jnp.float32)
    return summed

def conv_flip(padded, kernel, lon_rows, lat_cols):
    summed = jnp.zeros((lon_rows, lat_cols, padded.shape[2]), jnp.float32)
    for i in range(7):
        for j in range(7):
            summed = summed + kernel[i * 7 + j] * padded[6 - i:6 - i + lon_rows, 6 - j:6 - j + lat_cols]
    return summed

def model_step(state_field, weights):
    lift_weight, conv_kernel, norm_gain, up_weight, down_weight, out_weight = weights
    channels, lon_rows, lat_cols = state_field.shape
    hidden = lift_weight.shape[1]
    state_half = state_field.astype(jnp.bfloat16).reshape(channels, lon_rows * lat_cols)
    lifted = half_dot(state_half.T, lift_weight).astype(jnp.bfloat16)
    lifted = lifted.reshape(lon_rows, lat_cols, hidden)
    mixed_taps = conv_taps(wrap_pad(lifted, 3), conv_kernel, lon_rows, lat_cols)
    center = mixed_taps - lax.optimization_barrier(jnp.mean(mixed_taps, axis=2, keepdims=True))
    inverse = lax.rsqrt(lax.optimization_barrier(jnp.mean(center * center, axis=2, keepdims=True)) + eps_norm)
    normal = center * inverse
    normed = (normal * norm_gain).astype(jnp.bfloat16)

    def mlp_block(pieces):
        normed_part, lifted_part = pieces
        middle = half_dot(normed_part, up_weight)
        active = gelu_value(middle).astype(jnp.bfloat16)
        return (lifted_part.astype(jnp.float32) + half_dot(active, down_weight)).astype(jnp.bfloat16)
    block_out = lax.map(mlp_block, (normed.reshape(N_LON, -1, hidden), lifted.reshape(N_LON, -1, hidden)))
    change = half_dot(block_out.reshape(lon_rows * lat_cols, hidden), out_weight)
    return (state_field + change.T.reshape(channels, lon_rows, lat_cols), (normal, inverse, normed))

def step_adjoint(cotangent, saved, weights):
    lift_weight, conv_kernel, norm_gain, up_weight, down_weight, out_weight = weights
    normal, inverse, normed = saved
    channels, lon_rows, lat_cols = cotangent.shape
    hidden = lift_weight.shape[1]
    cot_half = cotangent.astype(jnp.bfloat16).reshape(channels, lon_rows * lat_cols)
    g_block = half_dot(cot_half.T, out_weight.T)

    def back_block(pieces):
        normed_part, block_part = pieces
        middle = half_dot(normed_part, up_weight)
        g_active = half_dot(block_part.astype(jnp.bfloat16), down_weight.T)
        g_middle = (g_active * gelu_slope(middle)).astype(jnp.bfloat16)
        return half_dot(g_middle, up_weight.T)
    g_normed = lax.map(back_block, (normed.reshape(N_LON, -1, hidden), g_block.reshape(N_LON, -1, hidden)))
    g_normed = g_normed.reshape(lon_rows, lat_cols, hidden)
    g_scaled = g_normed * norm_gain
    g_mixed = inverse * (g_scaled - lax.optimization_barrier(jnp.mean(g_scaled, axis=2, keepdims=True)) - normal * lax.optimization_barrier(jnp.mean(g_scaled * normal, axis=2, keepdims=True)))
    g_lifted = g_block.reshape(lon_rows, lat_cols, hidden) + conv_flip(wrap_pad(g_mixed, 3), conv_kernel, lon_rows, lat_cols)
    g_state = half_dot(g_lifted.reshape(lon_rows * lat_cols, hidden).astype(jnp.bfloat16), lift_weight.T)
    return cotangent + g_state.T.reshape(channels, lon_rows, lat_cols)

def tile_ops(cell_ids, point_weights):
    positions = jnp.arange(TILE_CELLS, dtype=jnp.int32)
    return lax.optimization_barrier(jnp.sum(point_weights[..., None] * (cell_ids[..., None] == positions).astype(jnp.float32), axis=2))

def to_tiles(state_field):
    channels, lon_rows, lat_cols = state_field.shape
    split = state_field.reshape(channels, N_LON, LON_DEV, TILES, TILE_LAT)
    return split.transpose(1, 3, 0, 2, 4).reshape(N_LON * TILES, channels, TILE_CELLS)

def from_tiles(tile_sums):
    channels = tile_sums.shape[1]
    split = tile_sums.reshape(N_LON, TILES, channels, LON_DEV, TILE_LAT)
    return split.transpose(2, 0, 3, 1, 4).reshape(channels, N_LON * LON_DEV, LAT)

def misfit_of(state_field, moment, operator, obs_owner, tile_counts, obs_values, obs_precision):
    channels = state_field.shape[0]
    model_equiv = jnp.einsum('gkc,gsc->gks', operator, to_tiles(state_field), precision=highest).reshape(-1, channels)
    per_band = TILES * K
    owner_ids = obs_owner[moment, :, 0]
    grouped = owner_ids.reshape(N_LON, per_band)
    onehot = (grouped[:, :, None] == jnp.arange(N_LON, dtype=jnp.int32)).astype(jnp.int32)
    before = jnp.cumsum(onehot, axis=1) - onehot
    place = lax.optimization_barrier(jnp.sum(before * onehot, axis=2)).reshape(-1).astype(jnp.int32)
    source = (jnp.arange(N_LON * per_band, dtype=jnp.int32) // per_band).astype(jnp.int32)
    target = obs_values[moment][owner_ids, source, place]
    weight_obs = obs_precision[moment][owner_ids, source, place]
    live_slots = (jnp.arange(K, dtype=jnp.int32)[None, :] < tile_counts[moment][:, None]).astype(jnp.float32).reshape(-1, 1)
    return live_slots * (weight_obs * (model_equiv - target))

def pull_back(operator, misfit):
    channels = misfit.shape[1]
    tile_sums = jnp.einsum('gkc,gks->gsc', operator, misfit.reshape(-1, K, channels), precision=highest)
    return from_tiles(tile_sums)

def reference(state_start, lift_weight, conv_kernel, norm_gain, up_weight, down_weight, out_weight, obs_cells, obs_weights, tile_counts, obs_owner, obs_values, obs_precision):
    weights = (lift_weight, conv_kernel, norm_gain, up_weight, down_weight, out_weight)
    state_one, saved_zero = model_step(state_start, weights)
    state_two, saved_one = model_step(state_one, weights)
    operator_one = tile_ops(obs_cells[0], obs_weights[0])
    operator_two = tile_ops(obs_cells[1], obs_weights[1])
    misfit_one = misfit_of(state_one, 0, operator_one, obs_owner, tile_counts, obs_values, obs_precision)
    misfit_two = misfit_of(state_two, 1, operator_two, obs_owner, tile_counts, obs_values, obs_precision)
    carried = step_adjoint(pull_back(operator_two, misfit_two), saved_one, weights) + pull_back(operator_one, misfit_one)
    return step_adjoint(carried, saved_zero, weights)
```

```python
import jax
import jax.numpy as jnp
from jax import lax
from jax.experimental import pallas as pl
from jax.experimental.pallas import tpu as pltpu
from jax.sharding import PartitionSpec as P

gelu_coef = 0.044715
root_two_pi = 0.7978845608028654
eps_norm = 1e-06
TAPS = 7
REACH = 3
BLOCKS = 8
TILE_LAT = 8
LANES = 128
VMEM_LIMIT = 60 * 1024 * 1024
f32, bf16 = jnp.float32, jnp.bfloat16
ACROSS = (((1,), (1,)), ((), ()))
DOWN = (((0,), (0,)), ((), ()))


def send_rows(ref, sems, at):
    send_sem, recv_sem = sems
    rows = ref.shape[0] - 2 * REACH
    count = lax.axis_size("lon")
    here = lax.axis_index("lon")
    ahead, behind = lax.rem(here + 1, count), lax.rem(here + count - 1, count)
    copies = []
    for side, (start, into, target) in enumerate(
        ((rows, 0, ahead), (REACH, rows + REACH, behind))
    ):
        copy = pltpu.make_async_remote_copy(
            src_ref=ref.at[pl.ds(start, REACH)],
            dst_ref=ref.at[pl.ds(into, REACH)],
            send_sem=send_sem.at[2 * at + side],
            recv_sem=recv_sem.at[2 * at + side],
            device_id={"lon": target},
            device_id_type=pl.DeviceIdType.MESH,
        )
        copy.start()
        copies.append(copy)
    return copies


def put_tiles(xp_ref, row, values):
    runs = values.shape[0] // BLOCKS
    tiles = values.reshape(runs, BLOCKS, values.shape[1])
    block = lax.broadcasted_iota(jnp.int32, (REACH, BLOCKS, values.shape[1]), 1)
    xp_ref[row + REACH, REACH : REACH + runs] = tiles.astype(bf16)
    before = pltpu.roll(tiles[runs - REACH :], 1, 1)
    xp_ref[row + REACH, 0:REACH] = jnp.where(block == 0, 0.0, before).astype(bf16)
    after = pltpu.roll(tiles[:REACH], BLOCKS - 1, 1)
    xp_ref[row + REACH, REACH + runs :] = jnp.where(block == BLOCKS - 1, 0.0, after).astype(bf16)


def conv_tiles(xp_ref, kb_ref, o, start, number, flip):
    last = TAPS * TAPS - 1
    totals = [None] * number
    for i in range(TAPS):
        cells = [xp_ref[o + i, start + q] for q in range(number + TAPS - 1)]
        parts = [[] for _ in range(number)]
        for j in range(TAPS):
            tap = i * TAPS + j
            weight = kb_ref[last - tap if flip else tap]
            for q in range(number):
                parts[q].append(weight * cells[q + j])
                if j in (1, 3, 5):
                    top = parts[q].pop()
                    parts[q][-1] = parts[q][-1] + top
                if j == 3:
                    top = parts[q].pop()
                    parts[q][-1] = parts[q][-1] + top
                if j == 6:
                    top = parts[q].pop()
                    parts[q][-1] = parts[q][-1] + top
                    top = parts[q].pop()
                    parts[q][-1] = parts[q][-1] + top
        for q in range(number):
            term = parts[q][0].astype(f32)
            totals[q] = term if totals[q] is None else totals[q] + term
    return jnp.concatenate(totals, axis=0)


def whole_kernel(
    state_ref,
    lift_ref,
    kern_ref,
    gain_ref,
    up_ref,
    down_ref,
    outw_ref,
    idx_ref,
    wts_ref,
    code_ref,
    vals_ref,
    prec_ref,
    out_ref,
    tin_ref,
    nat_ref,
    kb_ref,
    xp0_ref,
    xp1_ref,
    xp2_ref,
    xp3_ref,
    one_ref,
    two_ref,
    cot_ref,
    normed_ref,
    normal_ref,
    inverse_ref,
    slope_ref,
    gblk_ref,
    op_ref,
    chosen_ref,
    sb_ref,
    rb_ref,
    send_sem,
    recv_sem,
    obs_send,
    obs_recv,
    own_sem,
):
    count = lax.axis_size("lon")
    here = lax.axis_index("lon")
    lon_rows = xp0_ref.shape[0] - 2 * REACH
    runs = xp0_ref.shape[1] - 2 * REACH
    lat_cols = runs * BLOCKS
    hidden = xp0_ref.shape[3]
    wide = up_ref.shape[1]
    channels = vals_ref.shape[-1]
    cap = sb_ref.shape[1] // 2
    slots = code_ref.shape[1]
    sems = (send_sem, recv_sem)
    group = lon_rows // 4
    rows = group * lat_cols
    barrier = pltpu.get_barrier_semaphore()

    def peer(step):
        return lax.rem(here + step, count)

    def greet(step, carry):
        pl.semaphore_signal(
            barrier, inc=1, device_id={"lon": peer(step)}, device_id_type=pl.DeviceIdType.MESH
        )
        return carry

    lax.fori_loop(1, count, greet, 0)

    tin_ref[...] = jnp.zeros_like(tin_ref)

    def tap_row(tap, carry):
        row = kern_ref[pl.ds(tap, 1), :]
        kb_ref[tap] = jnp.broadcast_to(row, (BLOCKS, hidden)).astype(bf16)
        return carry

    lax.fori_loop(0, TAPS * TAPS, tap_row, 0)

    def enter(o, carry):
        tin_ref[0:channels, :] = state_ref[pl.ds(o, channels, stride=lon_rows), :]
        nat_ref[...] = tin_ref[...].T
        base = pl.multiple_of(o * lat_cols, lat_cols)
        cells = jnp.concatenate(
            [nat_ref[pl.ds(r, BLOCKS, stride=runs), :] for r in range(runs)], axis=0
        )
        one_ref[pl.ds(base, lat_cols), :] = cells
        lifted = jnp.dot(cells.astype(bf16), lift_ref[...], preferred_element_type=f32)
        put_tiles(xp0_ref, o, lifted)
        return carry

    lax.fori_loop(0, lon_rows, enter, 0)

    def obs_row(band, carry):
        for moment in range(2):
            at = pl.ds(moment * cap, cap)
            for side, ref in enumerate((vals_ref, prec_ref)):
                padded = jnp.concatenate(
                    [ref[moment, band], jnp.zeros((cap, LANES - channels), f32)], axis=1
                )
                sb_ref[band, at, side * LANES : (side + 1) * LANES] = padded.astype(bf16)
        return carry

    lax.fori_loop(0, count, obs_row, 0)

    pl.semaphore_wait(barrier, count - 1)
    halo = send_rows(xp0_ref, sems, 0)

    def obs_copy(step):
        return pltpu.make_async_remote_copy(
            src_ref=sb_ref.at[peer(step)],
            dst_ref=rb_ref.at[here],
            send_sem=obs_send.at[step - 1],
            recv_sem=obs_recv.at[step - 1],
            device_id={"lon": peer(step)},
            device_id_type=pl.DeviceIdType.MESH,
        )

    def obs_start(step, carry):
        obs_copy(step).start()
        return carry

    lax.fori_loop(1, count, obs_start, 0)
    own = pltpu.make_async_copy(sb_ref.at[here], rb_ref.at[here], own_sem)
    own.start()

    def obs_wait(step, carry):
        copy = obs_copy(step)
        copy.wait_send()
        pltpu.make_async_remote_copy(
            src_ref=sb_ref.at[peer(count - step)],
            dst_ref=rb_ref.at[peer(count - step)],
            send_sem=obs_send.at[step - 1],
            recv_sem=obs_recv.at[step - 1],
            device_id={"lon": peer(step)},
            device_id_type=pl.DeviceIdType.MESH,
        ).wait_recv()
        return carry

    def span(block):
        return pl.ds(pl.multiple_of(block * rows, rows), rows)


    def convolve(xp_ref, flip, finish, halo):
        number = runs // 2

        def at_row(o):
            for part in range(2):
                mixed = conv_tiles(xp_ref, kb_ref, o, part * number, number, flip)
                base = pl.multiple_of(o * lat_cols + part * number * BLOCKS, BLOCKS * number)
                finish(pl.ds(base, number * BLOCKS), mixed)

        def inner(o, carry):
            at_row(o)
            return carry

        def outer(k, carry):
            at_row(jnp.where(k < REACH, k, lon_rows - 2 * REACH + k))
            return carry

        lax.fori_loop(REACH, lon_rows - REACH, inner, 0)
        for copy in halo:
            copy.wait()
        lax.fori_loop(0, 2 * REACH, outer, 0)

    def edges_first(work, send):
        def first(k, carry):
            work(3 * k)
            return carry

        def second(k, carry):
            work(1 + k)
            return carry

        lax.fori_loop(0, 2, first, 0)
        copies = send()
        lax.fori_loop(0, 2, second, 0)
        return copies


    def forward(step, xp_ref, source_ref, target_ref, next_ref, halo):
        def finish(at, mixed):
            center = mixed - jnp.mean(mixed, axis=1, keepdims=True)
            inverse = lax.rsqrt(jnp.mean(center * center, axis=1, keepdims=True) + eps_norm)
            normal = center * inverse
            normal_ref[step, at, :] = normal.astype(bf16)
            normed_ref[at, :] = (normal * gain_ref[...]).astype(bf16)
            inverse_ref[step, at, :] = jnp.broadcast_to(inverse, (mixed.shape[0], LANES))

        convolve(xp_ref, False, finish, halo)

        def work(block):
            at = span(block)
            normed = normed_ref[at, :]
            lifted = xp_ref[pl.ds(REACH + block * group, group), REACH : REACH + runs]
            total = lifted.reshape(rows, hidden).astype(f32)
            piece = 256
            for start in range(0, wide, piece):
                cut = slice(start, start + piece)
                z = jnp.dot(normed, up_ref[:, cut], preferred_element_type=f32)
                square = z * z
                tanh_val = jnp.tanh(z * (root_two_pi + root_two_pi * gelu_coef * square))
                half = 0.5 + 0.5 * tanh_val
                active = (z * half).astype(bf16)
                rest = (1.0 - half).astype(bf16)
                share, arg = half.astype(bf16), z.astype(bf16)
                steep = bf16(6.0 * root_two_pi * gelu_coef)
                bend = arg * (bf16(2.0 * root_two_pi) + steep * (arg * arg))
                slope_ref[step, at, cut] = share + share * (rest * bend)
                total = total + jnp.dot(active, down_ref[cut, :], preferred_element_type=f32)
            change = jnp.dot(total.astype(bf16), outw_ref[...], preferred_element_type=f32)
            state = source_ref[at, :] + change
            target_ref[at, :] = state
            if next_ref is not None:
                lifted = jnp.dot(state.astype(bf16), lift_ref[...], preferred_element_type=f32)
                for k in range(group):
                    put_tiles(
                        next_ref, block * group + k, lifted[k * lat_cols : (k + 1) * lat_cols]
                    )

        return edges_first(work, lambda: send_rows(next_ref, sems, 1) if step == 0 else [])

    halo = forward(0, xp0_ref, one_ref, one_ref, xp1_ref, halo)
    forward(1, xp1_ref, one_ref, two_ref, None, halo)


    lax.fori_loop(1, count, obs_wait, 0)
    own.wait()

    def observe(moment, state, add):
        cells = lax.broadcasted_iota(jnp.int32, (lon_rows * runs, slots), 0)
        lines = jnp.zeros((lon_rows * runs, slots), f32)
        for p in range(idx_ref.shape[1]):
            hit = idx_ref[moment, p : p + 1, :] == cells
            lines = lines + jnp.where(hit, wts_ref[moment, p : p + 1, :], 0.0)
        op_ref[...] = lines.T.astype(bf16)
        places = count * cap
        code = code_ref[moment]
        select = (lax.broadcasted_iota(jnp.int32, (slots, places), 1) == code).astype(f32)
        data = rb_ref[:, moment * cap : (moment + 1) * cap, :].reshape(places, 2 * LANES)
        chosen_ref[...] = jnp.dot(select.astype(bf16), data, preferred_element_type=f32)
        each = slots // BLOCKS
        for block in range(BLOCKS):
            at = pl.ds(block, lon_rows * runs, stride=BLOCKS)
            mine = slice(block * each, (block + 1) * each)
            op = op_ref[mine, :]
            equiv = jnp.dot(op, state[at, :].astype(bf16), preferred_element_type=f32)
            misfit = chosen_ref[mine, LANES:] * (equiv - chosen_ref[mine, :LANES])
            pulled = lax.dot_general(op, misfit.astype(bf16), DOWN, preferred_element_type=f32)
            cot_ref[at, :] = cot_ref[at, :] + pulled if add else pulled


    def backward(step, xp_ref, target_ref):
        def work(block):
            at = span(block)
            g_block = lax.dot_general(
                cot_ref[at, :].astype(bf16), outw_ref[...], ACROSS, preferred_element_type=f32
            ).astype(bf16)
            gblk_ref[at, :] = g_block
            total = None
            piece = 256
            for start in range(0, wide, piece):
                cut = slice(start, start + piece)
                g_active = lax.dot_general(
                    g_block, down_ref[cut, :], ACROSS, preferred_element_type=f32
                )
                g_middle = g_active * slope_ref[step, at, cut].astype(f32)
                term = lax.dot_general(
                    g_middle.astype(bf16), up_ref[:, cut], ACROSS, preferred_element_type=f32
                )
                total = term if total is None else total + term
            g_scaled = total * gain_ref[...]
            normal = normal_ref[step, at, :].astype(f32)
            g_mixed = inverse_ref[step, at, 0:1] * (
                g_scaled
                - jnp.mean(g_scaled, axis=1, keepdims=True)
                - normal * jnp.mean(g_scaled * normal, axis=1, keepdims=True)
            )
            for k in range(group):
                put_tiles(xp_ref, block * group + k, g_mixed[k * lat_cols : (k + 1) * lat_cols])

        halo = edges_first(work, lambda: send_rows(xp_ref, sems, 3 - step))

        def finish(at, summed):
            g_lifted = (gblk_ref[at, :].astype(f32) + summed).astype(bf16)
            g_state = lax.dot_general(g_lifted, lift_ref[...], ACROSS, preferred_element_type=f32)
            target_ref[at, :] = cot_ref[at, :] + g_state

        convolve(xp_ref, True, finish, halo)

    observe(1, two_ref, False)
    backward(1, xp2_ref, cot_ref)
    observe(0, one_ref, True)
    backward(0, xp3_ref, out_ref)


def shards(
    state_start,
    lift_weight,
    conv_kernel,
    norm_gain,
    up_weight,
    down_weight,
    out_weight,
    obs_cells,
    obs_weights,
    tile_counts,
    obs_owner,
    obs_values,
    obs_precision,
):
    channels, lon_rows, lat_cols = state_start.shape
    hidden, wide = up_weight.shape
    runs = lat_cols // BLOCKS
    count, cap = obs_values.shape[2:4]
    tiles, slot_total, points = obs_cells.shape[1:]
    slots = tiles * slot_total
    amount = lon_rows * lat_cols

    first = (jnp.arange(tiles, dtype=jnp.int32) * TILE_LAT) % runs
    idx = (obs_cells // TILE_LAT) * runs + first[None, :, None, None] + obs_cells % TILE_LAT
    by_point = lambda a: a.transpose(0, 3, 1, 2).reshape(2, points, slots)

    owner = obs_owner[:, :, 0]
    hit = owner[:, :, None] == jnp.arange(count, dtype=jnp.int32)
    at = jnp.arange(slots, dtype=jnp.int32)
    earlier = (at[None, :] < at[:, None]).astype(bf16)
    before = jnp.einsum("qp,tpn->tqn", earlier, hit.astype(bf16), preferred_element_type=f32)
    place = jnp.sum(jnp.where(hit, before, 0.0), axis=2).astype(jnp.int32)
    live = jnp.arange(slot_total, dtype=jnp.int32) < tile_counts[:, :, None]
    code = jnp.where(live.reshape(2, slots), owner * cap + place, -1)[:, :, None]

    vmem = pl.BlockSpec(memory_space=pltpu.VMEM)
    field = (lon_rows + 2 * REACH, runs + 2 * REACH, BLOCKS, hidden)
    result = pl.pallas_call(
        whole_kernel,
        out_shape=jax.ShapeDtypeStruct((amount, LANES), f32),
        in_specs=[vmem] * 12,
        out_specs=vmem,
        scratch_shapes=[
            pltpu.VMEM((LANES, LANES), f32),
            pltpu.VMEM((LANES, LANES), f32),
            pltpu.VMEM((TAPS * TAPS, BLOCKS, hidden), bf16),
            *[pltpu.VMEM(field, bf16)] * 4,
            *[pltpu.VMEM((amount, LANES), f32)] * 3,
            pltpu.VMEM((amount, hidden), bf16),
            pltpu.VMEM((2, amount, hidden), bf16),
            pltpu.VMEM((2, amount, LANES), f32),
            pltpu.VMEM((2, amount, wide), bf16),
            pltpu.VMEM((amount, hidden), bf16),
            pltpu.VMEM((slots, lon_rows * runs), bf16),
            pltpu.VMEM((slots, 2 * LANES), f32),
            pltpu.VMEM((count, 2 * cap, 2 * LANES), bf16),
            pltpu.VMEM((count, 2 * cap, 2 * LANES), bf16),
            pltpu.SemaphoreType.DMA((8,)),
            pltpu.SemaphoreType.DMA((8,)),
            pltpu.SemaphoreType.DMA((count - 1,)),
            pltpu.SemaphoreType.DMA((count - 1,)),
            pltpu.SemaphoreType.DMA,
        ],
        compiler_params=pltpu.CompilerParams(
            vmem_limit_bytes=VMEM_LIMIT, collective_id=0, has_side_effects=True
        ),
    )(
        state_start.reshape(channels * lon_rows, lat_cols),
        jnp.pad(lift_weight, ((0, LANES - channels), (0, 0))),
        conv_kernel,
        norm_gain.reshape(1, hidden),
        up_weight,
        down_weight,
        jnp.pad(out_weight, ((0, 0), (0, LANES - channels))),
        by_point(idx),
        by_point(obs_weights),
        code,
        obs_values[:, 0],
        obs_precision[:, 0],
    )
    split = result.reshape(lon_rows, runs, BLOCKS, LANES)[..., :channels]
    return split.transpose(3, 0, 2, 1).reshape(channels, lon_rows, lat_cols)


def solution(mesh):
    placed = (
        P("member", "lon", None),
        P(),
        P(),
        P(),
        P(),
        P(),
        P(),
        P("member", "lon", None, None),
        P("member", "lon", None, None),
        P("member", "lon"),
        P("member", "lon", None),
        P("member", "lon", None, None, None),
        P("member", "lon", None, None, None),
    )
    return jax.shard_map(
        shards, mesh=mesh, in_specs=placed, out_specs=P("member", "lon", None), check_vma=False
    )
```

```python
import jax
import jax.numpy as jnp
from jax import lax
from jax.experimental import pallas as pl
from jax.experimental.pallas import tpu as pltpu
from jax.sharding import PartitionSpec as P

gelu_coef = 0.044715
root_two_pi = 0.7978845608028654
eps_norm = 1e-06
TAPS = 7
REACH = 3
BLOCKS = 8
TILE_LAT = 8
LANES = 128
VMEM_LIMIT = 60 * 1024 * 1024
f32, bf16 = jnp.float32, jnp.bfloat16
ACROSS = (((1,), (1,)), ((), ()))
DOWN = (((0,), (0,)), ((), ()))


def halo_copies(ref, sems, at):
    send_sem, recv_sem = sems
    rows = ref.shape[0] - 2 * REACH
    runs = pl.ds(REACH, ref.shape[1] - 2 * REACH)
    count = lax.axis_size("lon")
    here = lax.axis_index("lon")
    ahead, behind = lax.rem(here + 1, count), lax.rem(here + count - 1, count)
    return [
        pltpu.make_async_remote_copy(
            src_ref=ref.at[pl.ds(start, REACH), runs],
            dst_ref=ref.at[pl.ds(into, REACH), runs],
            send_sem=send_sem.at[2 * at + side],
            recv_sem=recv_sem.at[2 * at + side],
            device_id={"lon": target},
            device_id_type=pl.DeviceIdType.MESH,
        )
        for side, (start, into, target) in enumerate(
            ((rows, 0, ahead), (REACH, rows + REACH, behind))
        )
    ]


def put_ends(xp_ref, at, low, high):
    block = lax.broadcasted_iota(jnp.int32, low.shape, 1)
    runs = xp_ref.shape[1] - 2 * REACH
    before = pltpu.roll(high, 1, 1)
    xp_ref[at, 0:REACH] = jnp.where(block == 0, 0.0, before).astype(bf16)
    after = pltpu.roll(low, BLOCKS - 1, 1)
    xp_ref[at, REACH + runs :] = jnp.where(block == BLOCKS - 1, 0.0, after).astype(bf16)


def put_tiles(xp_ref, row, values):
    runs = values.shape[0] // BLOCKS
    tiles = values.reshape(runs, BLOCKS, values.shape[1])
    xp_ref[row + REACH, REACH : REACH + runs] = tiles.astype(bf16)
    put_ends(xp_ref, row + REACH, tiles[:REACH], tiles[runs - REACH :])


def tree(terms):
    while len(terms) > 1:
        terms = [
            terms[k] + terms[k + 1] if k + 1 < len(terms) else terms[k]
            for k in range(0, len(terms), 2)
        ]
    return terms[0]


def conv_row(xp_ref, kb_ref, mix_ref, o, flip):
    runs = mix_ref.shape[1]
    last = TAPS * TAPS - 1
    for first in range(0, TAPS, 2):
        lines = range(first, min(first + 2, TAPS))
        weights = {}
        for i in lines:
            for j in range(TAPS):
                tap = i * TAPS + j
                weights[i, j] = kb_ref[last - tap if flip else tap]
        window = {i: [xp_ref[o + i, q] for q in range(TAPS - 1)] for i in lines}
        for r in range(runs):
            sums = []
            for i in lines:
                window[i].append(xp_ref[o + i, r + TAPS - 1])
                sums.append(tree([weights[i, j] * window[i][j] for j in range(TAPS)]))
                window[i].pop(0)
            term = tree(sums).astype(f32)
            mix_ref[o, r] = term if first == 0 else mix_ref[o, r] + term


def whole_kernel(
    state_ref,
    lift_ref,
    kern_ref,
    gain_ref,
    up_ref,
    down_ref,
    outw_ref,
    cell_ref,
    wts_ref,
    limit_ref,
    owner_ref,
    vals_ref,
    prec_ref,
    out_ref,
    tin_ref,
    nat_ref,
    pad_ref,
    liftp_ref,
    outp_ref,
    kb_ref,
    xp0_ref,
    xp1_ref,
    xp2_ref,
    xp3_ref,
    one_ref,
    two_ref,
    cot_ref,
    pull_ref,
    mix_ref,
    normal_ref,
    inverse_ref,
    slope_ref,
    gblk_ref,
    code_ref,
    op_ref,
    chosen_ref,
    sb_ref,
    rb_ref,
    send_sem,
    recv_sem,
    obs_send,
    obs_recv,
    own_sem,
):
    count = lax.axis_size("lon")
    here = lax.axis_index("lon")
    lon_rows, runs, _, hidden = mix_ref.shape
    lat_cols = runs * BLOCKS
    wide = up_ref.shape[1]
    channels = vals_ref.shape[-1]
    cap = vals_ref.shape[2]
    tiles, points, each = cell_ref.shape[1:]
    slots = tiles * each
    sems = (send_sem, recv_sem)
    quarter = lon_rows // 4
    inner = ((quarter, lon_rows - quarter),)
    edges = ((0, quarter), (lon_rows - quarter, lon_rows))
    barrier = pltpu.get_barrier_semaphore()
    ones = jnp.full((hidden, LANES), 1.0 / hidden, bf16)

    def peer(step):
        return lax.rem(here + step, count)

    def greet(step, carry):
        pl.semaphore_signal(
            barrier, inc=1, device_id={"lon": peer(step)}, device_id_type=pl.DeviceIdType.MESH
        )
        return carry

    lax.fori_loop(1, count, greet, 0)


    for ref, into_ref in ((lift_ref, liftp_ref), (outw_ref, outp_ref)):
        pad_ref[...] = jnp.zeros_like(pad_ref)
        pad_ref[0:channels, :] = ref[...].astype(f32)
        into_ref[...] = pad_ref[...].astype(bf16)

    tin_ref[...] = jnp.zeros_like(tin_ref)

    def tap_row(tap, carry):
        row = kern_ref[pl.ds(tap, 1), :]
        kb_ref[tap] = jnp.broadcast_to(row, (BLOCKS, hidden)).astype(bf16)
        return carry

    lax.fori_loop(0, TAPS * TAPS, tap_row, 0)

    def enter(o, carry):
        tin_ref[0:channels, :] = state_ref[pl.ds(o, channels, stride=lon_rows), :]
        nat_ref[...] = tin_ref[...].T
        base = pl.multiple_of(o * lat_cols, lat_cols)
        cells = jnp.concatenate(
            [nat_ref[pl.ds(r, BLOCKS, stride=runs), :] for r in range(runs)], axis=0
        )
        one_ref[pl.ds(base, lat_cols), :] = cells
        lifted = jnp.dot(cells.astype(bf16), liftp_ref[...], preferred_element_type=f32)
        put_tiles(xp0_ref, o, lifted)
        return carry

    lax.fori_loop(0, lon_rows, enter, 0)


    def obs_row(band, carry):
        for moment in range(2):
            for side, ref in enumerate((vals_ref, prec_ref)):
                padded = jnp.concatenate(
                    [ref[moment, band], jnp.zeros((cap, LANES - channels), f32)], axis=1
                )
                sb_ref[moment, band, :, side * LANES : (side + 1) * LANES] = padded.astype(bf16)
        return carry

    lax.fori_loop(0, count, obs_row, 0)


    def lookup(moment):
        owner = owner_ref[moment]
        column = jnp.broadcast_to(owner.astype(f32), (LANES, slots)).T
        pieces = []
        for part in range(slots // LANES):
            row = owner[:, part * LANES : (part + 1) * LANES]
            earlier = lax.broadcasted_iota(jnp.int32, (slots, LANES), 0)
            later = lax.broadcasted_iota(jnp.int32, (slots, LANES), 1) + part * LANES
            same = (column == row.astype(f32)) & (earlier < later)
            place = jnp.sum(jnp.where(same, 1.0, 0.0), axis=0, keepdims=True)
            lane = lax.broadcasted_iota(jnp.int32, (1, LANES), 1)
            limit = jnp.zeros((1, LANES), jnp.int32)
            for k in range(LANES // each):
                tile = part * (LANES // each) + k
                limit = jnp.where(lane >= k * each, limit_ref[moment, tile] + k * each, limit)
            code = row.astype(f32) * cap + place
            pieces.append(jnp.where(lane < limit, code, -1.0))
        code = jnp.concatenate(pieces, axis=1)
        code_ref[moment] = jnp.broadcast_to(code, (LANES, slots)).T

    lookup(0)
    lookup(1)

    pl.semaphore_wait(barrier, count - 1)

    def send(ref, at):
        for copy in halo_copies(ref, sems, at):
            copy.start()

    def arrive(ref, at):
        for copy in halo_copies(ref, sems, at):
            copy.wait()

        def ends(k, carry):
            row = jnp.where(k < REACH, k, lon_rows + k)
            low = ref[row, REACH : 2 * REACH].astype(f32)
            high = ref[row, runs : runs + REACH].astype(f32)
            put_ends(ref, row, low, high)
            return carry

        lax.fori_loop(0, 2 * REACH, ends, 0)

    def obs_copy(moment, step, band):
        return pltpu.make_async_remote_copy(
            src_ref=sb_ref.at[moment, band],
            dst_ref=rb_ref.at[moment, here],
            send_sem=obs_send.at[moment, step - 1],
            recv_sem=obs_recv.at[moment, step - 1],
            device_id={"lon": peer(step)},
            device_id_type=pl.DeviceIdType.MESH,
        )

    def own_copy(moment):
        return pltpu.make_async_copy(
            sb_ref.at[moment, here], rb_ref.at[moment, here], own_sem.at[moment]
        )

    def obs_start(moment):
        def start(step, carry):
            obs_copy(moment, step, peer(step)).start()
            return carry

        lax.fori_loop(1, count, start, 0)
        own_copy(moment).start()

    def obs_wait(moment):
        def wait(step, carry):
            obs_copy(moment, step, peer(step)).wait_send()
            source = peer(count - step)
            pltpu.make_async_remote_copy(
                src_ref=sb_ref.at[moment, source],
                dst_ref=rb_ref.at[moment, source],
                send_sem=obs_send.at[moment, step - 1],
                recv_sem=obs_recv.at[moment, step - 1],
                device_id={"lon": peer(step)},
                device_id_type=pl.DeviceIdType.MESH,
            ).wait_recv()
            return carry

        lax.fori_loop(1, count, wait, 0)
        own_copy(moment).wait()


    def take(load, part):
        chunks = [load(a, b) for a, b in part]
        return chunks[0] if len(chunks) == 1 else jnp.concatenate(chunks, axis=0)

    def cells(ref):
        return lambda a, b: ref[a * lat_cols : b * lat_cols, :]

    def leading(ref, step):
        return lambda a, b: ref[step, a * lat_cols : b * lat_cols, :]

    def put(ref, part, values, step=None):
        at = 0
        for a, b in part:
            size = (b - a) * lat_cols
            where = slice(a * lat_cols, b * lat_cols)
            if step is None:
                ref[where, :] = values[at : at + size]
            else:
                ref[step, where, :] = values[at : at + size]
            at += size

    def put_field(xp_ref, part, values):
        at = 0
        for a, b in part:
            for o in range(a, b):
                put_tiles(xp_ref, o, values[at : at + lat_cols])
                at += lat_cols

    def sums(part):
        return take(
            lambda a, b: mix_ref[a:b].reshape((b - a) * lat_cols, hidden),
            part,
        )

    def mean(values):
        wide_mean = jnp.dot(values.astype(bf16), ones, preferred_element_type=f32)
        return jnp.concatenate([wide_mean] * (hidden // LANES), axis=1)

    def conv_inner(xp_ref, flip):
        def body(o, carry):
            conv_row(xp_ref, kb_ref, mix_ref, o, flip)
            return carry

        lax.fori_loop(REACH, lon_rows - REACH, body, 0)

    def conv_outer(xp_ref, flip):
        def body(k, carry):
            o = jnp.where(k < REACH, k, lon_rows - 2 * REACH + k)
            conv_row(xp_ref, kb_ref, mix_ref, o, flip)
            return carry

        lax.fori_loop(0, 2 * REACH, body, 0)

    def forward(step, part, xp_ref, source_ref, target_ref, next_ref):
        mixed = sums(part)
        center = mixed - mean(mixed)
        inverse = lax.rsqrt(mean(center * center) + eps_norm)
        normal = center * inverse
        put(normal_ref, part, normal.astype(bf16), step)
        put(inverse_ref, part, inverse[:, :LANES], step)
        normed = (normal * gain_ref[...]).astype(bf16)
        total = take(
            lambda a, b: xp_ref[a + REACH : b + REACH, REACH : REACH + runs]
            .reshape((b - a) * lat_cols, hidden)
            .astype(f32),
            part,
        )
        piece = 256
        one = bf16(root_two_pi)
        three = bf16(root_two_pi * gelu_coef)
        half_one = bf16(0.5)
        for start in range(0, wide, piece):
            cut = slice(start, start + piece)
            z = jnp.dot(normed, up_ref[:, cut], preferred_element_type=f32).astype(bf16)
            square = z * z
            tanh_val = jnp.tanh(z * (one + three * square))
            share = half_one + half_one * tanh_val
            active = z * share
            rest = bf16(1.0) - share
            bend = z * (bf16(2.0) * one + bf16(6.0) * three * square)
            slope = share + share * (rest * bend)
            at = 0
            for a, b in part:
                size = (b - a) * lat_cols
                slope_ref[step, a * lat_cols : b * lat_cols, cut] = slope[at : at + size]
                at += size
            total = total + jnp.dot(active, down_ref[cut, :], preferred_element_type=f32)
        change = lax.dot_general(
            total.astype(bf16), outp_ref[...], ACROSS, preferred_element_type=f32
        )
        state = take(cells(source_ref), part) + change
        put(target_ref, part, state)
        if next_ref is not None:
            lifted = jnp.dot(state.astype(bf16), liftp_ref[...], preferred_element_type=f32)
            put_field(next_ref, part, lifted)

    def observe(moment, state_ref, target_ref):
        spots = lon_rows * runs
        by_point = lambda ref: jnp.concatenate([ref[moment, g] for g in range(tiles)], axis=1)
        cell = by_point(cell_ref)
        lane = lax.broadcasted_iota(jnp.int32, (points, slots), 1)
        first = ((lane // each) * TILE_LAT) % runs
        spot = (cell // TILE_LAT) * runs + first + cell % TILE_LAT
        weight = by_point(wts_ref)
        number = lax.broadcasted_iota(jnp.int32, (spots, slots), 0)
        lines = jnp.zeros((spots, slots), f32)
        for p in range(points):
            hit = spot[p : p + 1, :] == number
            lines = lines + jnp.where(hit, weight[p : p + 1, :], 0.0)
        op_ref[...] = lines.T.astype(bf16)
        places = count * cap
        code = code_ref[moment]
        line = lax.broadcasted_iota(jnp.int32, (slots, LANES), 1).astype(f32)
        select = jnp.concatenate(
            [
                jnp.where(line + float(start) == code, 1.0, 0.0).astype(bf16)
                for start in range(0, places, LANES)
            ],
            axis=1,
        )
        data = rb_ref[moment].reshape(places, 2 * LANES)
        chosen_ref[...] = jnp.dot(select, data, preferred_element_type=f32)
        size = slots // BLOCKS
        for block in range(BLOCKS):
            at = pl.ds(block, spots, stride=BLOCKS)
            mine = slice(block * size, (block + 1) * size)
            op = op_ref[mine, :]
            equiv = jnp.dot(op, state_ref[at, :].astype(bf16), preferred_element_type=f32)
            misfit = chosen_ref[mine, LANES:] * (equiv - chosen_ref[mine, :LANES])
            target_ref[at, :] = lax.dot_general(
                op, misfit.astype(bf16), DOWN, preferred_element_type=f32
            )

    def gathered(part):
        g_lifted = (take(cells(gblk_ref), part).astype(f32) + sums(part)).astype(bf16)
        g_state = lax.dot_general(g_lifted, liftp_ref[...], ACROSS, preferred_element_type=f32)
        return take(cells(cot_ref), part) + g_state

    def backward(step, part, xp_ref, cotangent):
        g_block = jnp.dot(cotangent.astype(bf16), outp_ref[...], preferred_element_type=f32)
        g_block = g_block.astype(bf16)
        put(gblk_ref, part, g_block)
        total = None
        piece = 256
        for start in range(0, wide, piece):
            cut = slice(start, start + piece)
            g_active = lax.dot_general(
                g_block, down_ref[cut, :], ACROSS, preferred_element_type=f32
            )
            slope = take(lambda a, b: slope_ref[step, a * lat_cols : b * lat_cols, cut], part)
            term = lax.dot_general(
                g_active.astype(bf16) * slope, up_ref[:, cut], ACROSS, preferred_element_type=f32
            )
            total = term if total is None else total + term
        g_scaled = total * gain_ref[...]
        normal = take(leading(normal_ref, step), part).astype(f32)
        inverse = take(leading(inverse_ref, step), part)
        inverse = jnp.concatenate([inverse] * (hidden // LANES), axis=1)
        g_mixed = inverse * (g_scaled - mean(g_scaled) - normal * mean(g_scaled * normal))
        put_field(xp_ref, part, g_mixed)

    def leave(part):
        put(cot_ref, part, gathered(part))
        for a, b in part:

            def body(o, carry):
                base = o * lat_cols
                rows = [cot_ref[pl.ds(base + k, runs, stride=BLOCKS), :] for k in range(BLOCKS)]
                turned = jnp.concatenate(rows, axis=0).T
                out_ref[pl.ds(o, channels, stride=lon_rows), :] = turned[:channels]
                return carry

            lax.fori_loop(a, b, body, 0)


    send(xp0_ref, 0)
    obs_start(1)
    conv_inner(xp0_ref, False)
    forward(0, inner, xp0_ref, one_ref, one_ref, xp1_ref)
    arrive(xp0_ref, 0)
    conv_outer(xp0_ref, False)
    forward(0, edges, xp0_ref, one_ref, one_ref, xp1_ref)
    send(xp1_ref, 1)
    conv_inner(xp1_ref, False)
    forward(1, inner, xp1_ref, one_ref, two_ref, None)
    arrive(xp1_ref, 1)
    obs_start(0)
    conv_outer(xp1_ref, False)
    forward(1, edges, xp1_ref, one_ref, two_ref, None)
    obs_wait(1)
    observe(1, two_ref, cot_ref)
    backward(1, edges, xp2_ref, take(cells(cot_ref), edges))
    send(xp2_ref, 2)
    backward(1, inner, xp2_ref, take(cells(cot_ref), inner))
    conv_inner(xp2_ref, True)
    obs_wait(0)
    observe(0, one_ref, pull_ref)
    arrive(xp2_ref, 2)
    conv_outer(xp2_ref, True)

    def carried(part):
        value = gathered(part) + take(cells(pull_ref), part)
        put(cot_ref, part, value)
        return value

    backward(0, edges, xp3_ref, carried(edges))
    send(xp3_ref, 3)
    backward(0, inner, xp3_ref, carried(inner))
    conv_inner(xp3_ref, True)
    leave(inner)
    arrive(xp3_ref, 3)
    conv_outer(xp3_ref, True)
    leave(edges)


def shards(
    state_start,
    lift_weight,
    conv_kernel,
    norm_gain,
    up_weight,
    down_weight,
    out_weight,
    obs_cells,
    obs_weights,
    tile_counts,
    obs_owner,
    obs_values,
    obs_precision,
):
    channels, lon_rows, lat_cols = state_start.shape
    hidden, wide = up_weight.shape
    runs = lat_cols // BLOCKS
    count, cap = obs_values.shape[2:4]
    tiles, slot_total = obs_cells.shape[1:3]
    slots = tiles * slot_total
    amount = lon_rows * lat_cols

    vmem = pl.BlockSpec(memory_space=pltpu.VMEM)
    smem = pl.BlockSpec(memory_space=pltpu.SMEM)
    field = (lon_rows + 2 * REACH, runs + 2 * REACH, BLOCKS, hidden)
    result = pl.pallas_call(
        whole_kernel,
        out_shape=jax.ShapeDtypeStruct((channels * lon_rows, lat_cols), f32),
        in_specs=[vmem] * 9 + [smem] + [vmem] * 3,
        out_specs=vmem,
        scratch_shapes=[
            pltpu.VMEM((LANES, LANES), f32),
            pltpu.VMEM((LANES, LANES), f32),
            pltpu.VMEM((LANES, hidden), f32),
            pltpu.VMEM((LANES, hidden), bf16),
            pltpu.VMEM((LANES, hidden), bf16),
            pltpu.VMEM((TAPS * TAPS, BLOCKS, hidden), bf16),
            *[pltpu.VMEM(field, bf16)] * 4,
            *[pltpu.VMEM((amount, LANES), f32)] * 4,
            pltpu.VMEM((lon_rows, runs, BLOCKS, hidden), f32),
            pltpu.VMEM((2, amount, hidden), bf16),
            pltpu.VMEM((2, amount, LANES), f32),
            pltpu.VMEM((2, amount, wide), bf16),
            pltpu.VMEM((amount, hidden), bf16),
            pltpu.VMEM((2, slots, LANES), f32),
            pltpu.VMEM((slots, lon_rows * runs), bf16),
            pltpu.VMEM((slots, 2 * LANES), f32),
            pltpu.VMEM((2, count, cap, 2 * LANES), bf16),
            pltpu.VMEM((2, count, cap, 2 * LANES), bf16),
            pltpu.SemaphoreType.DMA((8,)),
            pltpu.SemaphoreType.DMA((8,)),
            pltpu.SemaphoreType.DMA((2, count - 1)),
            pltpu.SemaphoreType.DMA((2, count - 1)),
            pltpu.SemaphoreType.DMA((2,)),
        ],
        compiler_params=pltpu.CompilerParams(
            vmem_limit_bytes=VMEM_LIMIT, collective_id=0, has_side_effects=True
        ),
    )(
        state_start.reshape(channels * lon_rows, lat_cols),
        lift_weight,
        conv_kernel,
        norm_gain.reshape(1, hidden),
        up_weight,
        down_weight,
        out_weight.T,
        obs_cells.transpose(0, 1, 3, 2),
        obs_weights.transpose(0, 1, 3, 2),
        tile_counts,
        obs_owner.transpose(0, 2, 1),
        obs_values[:, 0],
        obs_precision[:, 0],
    )
    return result.reshape(channels, lon_rows, lat_cols)


def solution(mesh):
    placed = (
        P("member", "lon", None),
        P(),
        P(),
        P(),
        P(),
        P(),
        P(),
        P("member", "lon", None, None),
        P("member", "lon", None, None),
        P("member", "lon"),
        P("member", "lon", None),
        P("member", "lon", None, None, None),
        P("member", "lon", None, None, None),
    )
    return jax.shard_map(
        shards, mesh=mesh, in_specs=placed, out_specs=P("member", "lon", None), check_vma=False
    )
```

```python
import jax
import jax.numpy as jnp
from jax import lax
from jax.experimental import pallas as pl
from jax.experimental.pallas import tpu as pltpu
from jax.sharding import PartitionSpec as P

gelu_coef = 0.044715
root_two_pi = 0.7978845608028654
eps_norm = 1e-06
TAPS = 7
REACH = 3
BLOCKS = 8
TILE_LAT = 8
LANES = 128
VMEM_LIMIT = 60 * 1024 * 1024
f32, bf16 = jnp.float32, jnp.bfloat16
ACROSS = (((1,), (1,)), ((), ()))
DOWN = (((0,), (0,)), ((), ()))


def edge_copies(out_ref, in_ref, sems, at):
    send_sem, recv_sem = sems
    count = lax.axis_size("lon")
    here = lax.axis_index("lon")
    ahead, behind = lax.rem(here + 1, count), lax.rem(here + count - 1, count)
    return [
        pltpu.make_async_remote_copy(
            src_ref=out_ref.at[at, side],
            dst_ref=in_ref.at[at, 1 - side],
            send_sem=send_sem.at[2 * at + side],
            recv_sem=recv_sem.at[2 * at + 1 - side],
            device_id={"lon": target},
            device_id_type=pl.DeviceIdType.MESH,
        )
        for side, target in enumerate((behind, ahead))
    ]


def put_ends(xp_ref, at, low, high):
    block = lax.broadcasted_iota(jnp.int32, low.shape, 1)
    runs = xp_ref.shape[1] - 2 * REACH
    before = pltpu.roll(high, 1, 1)
    xp_ref[at, 0:REACH] = jnp.where(block == 0, 0.0, before).astype(bf16)
    after = pltpu.roll(low, BLOCKS - 1, 1)
    xp_ref[at, REACH + runs :] = jnp.where(block == BLOCKS - 1, 0.0, after).astype(bf16)


def put_tiles(xp_ref, row, values):
    runs = values.shape[0] // BLOCKS
    tiles = values.reshape(runs, BLOCKS, values.shape[1])
    xp_ref[row + REACH, REACH : REACH + runs] = tiles.astype(bf16)
    put_ends(xp_ref, row + REACH, tiles[:REACH], tiles[runs - REACH :])


def tree(terms):
    while len(terms) > 1:
        terms = [
            terms[k] + terms[k + 1] if k + 1 < len(terms) else terms[k]
            for k in range(0, len(terms), 2)
        ]
    return terms[0]


def conv_row(xp_ref, kb_ref, mix_ref, o, to, flip, taps=range(TAPS)):
    runs = mix_ref.shape[1]
    last = TAPS * TAPS - 1
    for first in range(0, len(taps), 2):
        lines = taps[first : first + 2]
        weights = {}
        for i in lines:
            for j in range(TAPS):
                tap = i * TAPS + j
                weights[i, j] = kb_ref[last - tap if flip else tap]
        window = {i: [xp_ref[o + i, q] for q in range(TAPS - 1)] for i in lines}
        for r in range(runs):
            sums = []
            for i in lines:
                window[i].append(xp_ref[o + i, r + TAPS - 1])
                sums.append(tree([weights[i, j] * window[i][j] for j in range(TAPS)]))
                window[i].pop(0)
            term = tree(sums).astype(f32)
            mix_ref[to, r] = term if first == 0 else mix_ref[to, r] + term


def whole_kernel(
    state_ref,
    lift_ref,
    kern_ref,
    gain_ref,
    up_ref,
    down_ref,
    outw_ref,
    cell_ref,
    wts_ref,
    limit_ref,
    owner_ref,
    vals_ref,
    prec_ref,
    out_ref,
    tin_ref,
    nat_ref,
    pad_ref,
    liftp_ref,
    outp_ref,
    kb_ref,
    xp0_ref,
    xp1_ref,
    xp2_ref,
    xp3_ref,
    one_ref,
    two_ref,
    cot_ref,
    pull_ref,
    mix_ref,
    normal_ref,
    inverse_ref,
    slope_ref,
    gblk_ref,
    land_ref,
    edge_ref,
    halo_ref,
    code_ref,
    op_ref,
    chosen_ref,
    late_ref,
    early_ref,
    late_in_ref,
    early_in_ref,
    send_sem,
    recv_sem,
    obs_send,
    obs_recv,
    own_sem,
):
    count = lax.axis_size("lon")
    here = lax.axis_index("lon")
    lon_rows, runs, _, hidden = mix_ref.shape
    lat_cols = runs * BLOCKS
    wide = up_ref.shape[1]
    channels = vals_ref.shape[-1]
    cap = vals_ref.shape[2]
    tiles, points, each = cell_ref.shape[1:]
    slots = tiles * each
    sems = (send_sem, recv_sem)
    quarter = lon_rows // 4
    inner = ((quarter, lon_rows - quarter),)
    edges = ((0, quarter), (lon_rows - quarter, lon_rows))
    barrier = pltpu.get_barrier_semaphore()
    ones = jnp.full((hidden, LANES), 1.0 / hidden, bf16)

    def peer(step):
        return lax.rem(here + step, count)

    def greet(step, carry):
        pl.semaphore_signal(
            barrier, inc=1, device_id={"lon": peer(step)}, device_id_type=pl.DeviceIdType.MESH
        )
        return carry

    lax.fori_loop(1, count, greet, 0)


    for ref, into_ref in ((lift_ref, liftp_ref), (outw_ref, outp_ref)):
        pad_ref[...] = jnp.zeros_like(pad_ref)
        pad_ref[0:channels, :] = ref[...].astype(f32)
        into_ref[...] = pad_ref[...].astype(bf16)

    tin_ref[...] = jnp.zeros_like(tin_ref)

    def tap_row(tap, carry):
        row = kern_ref[pl.ds(tap, 1), :]
        kb_ref[tap] = jnp.broadcast_to(row, (BLOCKS, hidden)).astype(bf16)
        return carry

    lax.fori_loop(0, TAPS * TAPS, tap_row, 0)

    def enter(o, carry):
        tin_ref[0:channels, :] = state_ref[pl.ds(o, channels, stride=lon_rows), :]
        nat_ref[...] = tin_ref[...].T
        base = pl.multiple_of(o * lat_cols, lat_cols)
        cells = jnp.concatenate(
            [nat_ref[pl.ds(r, BLOCKS, stride=runs), :] for r in range(runs)], axis=0
        )
        one_ref[pl.ds(base, lat_cols), :] = cells
        lifted = jnp.dot(cells.astype(bf16), liftp_ref[...], preferred_element_type=f32)
        put_tiles(xp0_ref, o, lifted)
        return carry

    lax.fori_loop(0, lon_rows, enter, 0)


    free = LANES - channels
    turns = [(channels - (channels - free * (2 - k))) % LANES for k in range(2)] + [channels]

    def obs_row(band, carry):
        filled = lambda part: jnp.concatenate(
            [part, jnp.zeros((cap, LANES - channels), f32)], axis=1
        )
        spare = filled(prec_ref[0, band])
        lane = lax.broadcasted_iota(jnp.int32, (cap, LANES), 1)
        for place, part in enumerate((vals_ref[1, band], prec_ref[1, band], vals_ref[0, band])):
            moved = pltpu.roll(spare, turns[place], 1)
            both = jnp.where(lane < channels, filled(part), moved)
            if place < 2:
                late_ref[band, :, place * LANES : (place + 1) * LANES] = both.astype(bf16)
            else:
                early_ref[band] = both.astype(bf16)
        return carry

    lax.fori_loop(0, count, obs_row, 0)


    def lookup(moment):
        owner = owner_ref[moment]
        column = jnp.broadcast_to(owner.astype(f32), (LANES, slots)).T
        pieces = []
        for part in range(slots // LANES):
            row = owner[:, part * LANES : (part + 1) * LANES]
            earlier = lax.broadcasted_iota(jnp.int32, (slots, LANES), 0)
            later = lax.broadcasted_iota(jnp.int32, (slots, LANES), 1) + part * LANES
            same = (column == row.astype(f32)) & (earlier < later)
            place = jnp.sum(jnp.where(same, 1.0, 0.0), axis=0, keepdims=True)
            lane = lax.broadcasted_iota(jnp.int32, (1, LANES), 1)
            limit = jnp.zeros((1, LANES), jnp.int32)
            for k in range(LANES // each):
                tile = part * (LANES // each) + k
                limit = jnp.where(lane >= k * each, limit_ref[moment, tile] + k * each, limit)
            code = row.astype(f32) * cap + place
            pieces.append(jnp.where(lane < limit, code, -1.0))
        code = jnp.concatenate(pieces, axis=1)
        code_ref[moment] = jnp.broadcast_to(code, (LANES, slots)).T

    lookup(0)
    lookup(1)

    pl.semaphore_wait(barrier, count - 1)

    strip = REACH * lat_cols
    total_rows = lon_rows * lat_cols

    def send(at, west, east):
        edge_ref[at, 0] = west.astype(bf16)
        edge_ref[at, 1] = east.astype(bf16)
        for copy in edge_copies(edge_ref, halo_ref, sems, at):
            copy.start()

    def send_state(at):
        send(at, one_ref[0:strip, :], one_ref[total_rows - strip :, :])

    def arrive(at):
        for copy in edge_copies(edge_ref, halo_ref, sems, at):
            copy.wait()

    def arrive_state(at, xp_ref):
        arrive(at)
        for side, first in enumerate((-REACH, lon_rows)):
            lifted = jnp.dot(halo_ref[at, side], liftp_ref[...], preferred_element_type=f32)
            for k in range(REACH):
                put_tiles(xp_ref, first + k, lifted[k * lat_cols : (k + 1) * lat_cols])

    boxes = ((early_ref, early_in_ref), (late_ref, late_in_ref))

    def obs_copy(moment, step, band):
        out_box, in_box = boxes[moment]
        return pltpu.make_async_remote_copy(
            src_ref=out_box.at[band],
            dst_ref=in_box.at[here],
            send_sem=obs_send.at[moment, step - 1],
            recv_sem=obs_recv.at[moment, step - 1],
            device_id={"lon": peer(step)},
            device_id_type=pl.DeviceIdType.MESH,
        )

    def own_copy(moment):
        out_box, in_box = boxes[moment]
        return pltpu.make_async_copy(out_box.at[here], in_box.at[here], own_sem.at[moment])

    def obs_start(moment):
        def start(step, carry):
            obs_copy(moment, step, peer(step)).start()
            return carry

        lax.fori_loop(1, count, start, 0)
        own_copy(moment).start()

    def obs_wait(moment):
        def wait(step, carry):
            obs_copy(moment, step, peer(step)).wait_send()
            source = peer(count - step)
            out_box, in_box = boxes[moment]
            pltpu.make_async_remote_copy(
                src_ref=out_box.at[source],
                dst_ref=in_box.at[source],
                send_sem=obs_send.at[moment, step - 1],
                recv_sem=obs_recv.at[moment, step - 1],
                device_id={"lon": peer(step)},
                device_id_type=pl.DeviceIdType.MESH,
            ).wait_recv()
            return carry

        lax.fori_loop(1, count, wait, 0)
        own_copy(moment).wait()


    def take(load, part):
        chunks = [load(a, b) for a, b in part]
        return chunks[0] if len(chunks) == 1 else jnp.concatenate(chunks, axis=0)

    def cells(ref):
        return lambda a, b: ref[a * lat_cols : b * lat_cols, :]

    def leading(ref, step):
        return lambda a, b: ref[step, a * lat_cols : b * lat_cols, :]

    def put(ref, part, values, step=None):
        at = 0
        for a, b in part:
            size = (b - a) * lat_cols
            where = slice(a * lat_cols, b * lat_cols)
            if step is None:
                ref[where, :] = values[at : at + size]
            else:
                ref[step, where, :] = values[at : at + size]
            at += size

    def put_field(xp_ref, part, values):
        at = 0
        for a, b in part:
            for o in range(a, b):
                put_tiles(xp_ref, o, values[at : at + lat_cols])
                at += lat_cols

    def sums(part):
        return take(
            lambda a, b: mix_ref[a:b].reshape((b - a) * lat_cols, hidden),
            part,
        )

    def mean(values):
        wide_mean = jnp.dot(values.astype(bf16), ones, preferred_element_type=f32)
        return jnp.concatenate([wide_mean] * (hidden // LANES), axis=1)

    def conv_inner(xp_ref, flip):
        def body(o, carry):
            conv_row(xp_ref, kb_ref, mix_ref, o, o, flip)
            return carry

        lax.fori_loop(REACH, lon_rows - REACH, body, 0)

    def conv_outer(xp_ref, flip):
        def body(k, carry):
            o = jnp.where(k < REACH, k, lon_rows - 2 * REACH + k)
            conv_row(xp_ref, kb_ref, mix_ref, o, o, flip)
            return carry

        lax.fori_loop(0, 2 * REACH, body, 0)

    def conv_own(xp_ref):
        for k in range(REACH):
            conv_row(xp_ref, kb_ref, mix_ref, k, k, True, range(REACH - k, TAPS))
            o = lon_rows - 1 - k
            conv_row(xp_ref, kb_ref, mix_ref, o, o, True, range(0, TAPS - REACH + k))

    def send_landing(at, xp_ref):
        for k in range(REACH):
            conv_row(xp_ref, kb_ref, land_ref, k - REACH, k, True, range(2 * REACH - k, TAPS))
            conv_row(xp_ref, kb_ref, land_ref, lon_rows + k, REACH + k, True, range(0, REACH - k))
        landed = land_ref[...].reshape(2 * strip, hidden).astype(bf16)
        g_state = lax.dot_general(landed, liftp_ref[...], ACROSS, preferred_element_type=f32)
        send(at, g_state[:strip], g_state[strip:])

    def forward(step, part, xp_ref, source_ref, target_ref, next_ref):
        mixed = sums(part)
        center = mixed - mean(mixed)
        inverse = lax.rsqrt(mean(center * center) + eps_norm)
        normal = center * inverse
        put(normal_ref, part, normal.astype(bf16), step)
        put(inverse_ref, part, inverse[:, :LANES], step)
        normed = (normal * gain_ref[...]).astype(bf16)
        total = take(
            lambda a, b: xp_ref[a + REACH : b + REACH, REACH : REACH + runs]
            .reshape((b - a) * lat_cols, hidden)
            .astype(f32),
            part,
        )
        piece = 256
        one = bf16(root_two_pi)
        three = bf16(root_two_pi * gelu_coef)
        half_one = bf16(0.5)
        for start in range(0, wide, piece):
            cut = slice(start, start + piece)
            z = jnp.dot(normed, up_ref[:, cut], preferred_element_type=f32).astype(bf16)
            square = z * z
            tanh_val = jnp.tanh(z * (one + three * square))
            share = half_one + half_one * tanh_val
            active = z * share
            rest = bf16(1.0) - share
            bend = z * (bf16(2.0) * one + bf16(6.0) * three * square)
            slope = share + share * (rest * bend)
            at = 0
            for a, b in part:
                size = (b - a) * lat_cols
                slope_ref[step, a * lat_cols : b * lat_cols, cut] = slope[at : at + size]
                at += size
            total = total + jnp.dot(active, down_ref[cut, :], preferred_element_type=f32)
        change = lax.dot_general(
            total.astype(bf16), outp_ref[...], ACROSS, preferred_element_type=f32
        )
        state = take(cells(source_ref), part) + change
        put(target_ref, part, state)
        if next_ref is not None:
            lifted = jnp.dot(state.astype(bf16), liftp_ref[...], preferred_element_type=f32)
            put_field(next_ref, part, lifted)

    def observe(moment, state_ref, target_ref):
        spots = lon_rows * runs
        by_point = lambda ref: jnp.concatenate([ref[moment, g] for g in range(tiles)], axis=1)
        cell = by_point(cell_ref)
        lane = lax.broadcasted_iota(jnp.int32, (points, slots), 1)
        first = ((lane // each) * TILE_LAT) % runs
        spot = (cell // TILE_LAT) * runs + first + cell % TILE_LAT
        weight = by_point(wts_ref)
        number = lax.broadcasted_iota(jnp.int32, (spots, slots), 0)
        lines = jnp.zeros((spots, slots), f32)
        for p in range(points):
            hit = spot[p : p + 1, :] == number
            lines = jnp.where(hit, lines + weight[p : p + 1, :], lines)
        op_ref[moment] = lines.T.astype(bf16)
        places = count * cap
        code = code_ref[moment]
        line = lax.broadcasted_iota(jnp.int32, (slots, LANES), 1).astype(f32)
        select = jnp.concatenate(
            [
                jnp.where(code - float(start) == line, 1.0, 0.0).astype(bf16)
                for start in range(0, places, LANES)
            ],
            axis=1,
        )
        data = late_in_ref[...].reshape(places, 2 * LANES)
        chosen = jnp.dot(select, data, preferred_element_type=f32)
        if moment == 0:
            data = early_in_ref[...].reshape(places, LANES)
            third = jnp.dot(select, data, preferred_element_type=f32)
            tiles3 = (chosen[:, :LANES], chosen[:, LANES:], third)
            back = [pltpu.roll(t, (LANES - n) % LANES, 1) for t, n in zip(tiles3, turns)]
            lane = lax.broadcasted_iota(jnp.int32, (slots, LANES), 1)
            start = channels - 2 * free
            weights = jnp.where(
                lane < start, back[2], jnp.where(lane < start + free, back[0], back[1])
            )
            weights = jnp.where(lane < channels, weights, 0.0)
            chosen = jnp.concatenate([third, weights], axis=1)
        chosen_ref[moment] = chosen
        size = slots // BLOCKS
        for block in range(BLOCKS):
            at = pl.ds(block, spots, stride=BLOCKS)
            mine = slice(block * size, (block + 1) * size)
            op = op_ref[moment, mine, :]
            equiv = jnp.dot(op, state_ref[at, :].astype(bf16), preferred_element_type=f32)
            chosen = chosen_ref[moment, mine, :]
            misfit = chosen[:, LANES:] * (equiv - chosen[:, :LANES])
            lane = lax.broadcasted_iota(jnp.int32, (size, LANES), 1)
            misfit = jnp.where(lane < channels, misfit, 0.0)
            target_ref[at, :] = lax.dot_general(
                op, misfit.astype(bf16), DOWN, preferred_element_type=f32
            )

    def gathered(part, at):
        g_lifted = (take(cells(gblk_ref), part).astype(f32) + sums(part)).astype(bf16)
        g_state = lax.dot_general(g_lifted, liftp_ref[...], ACROSS, preferred_element_type=f32)
        value = take(cells(cot_ref), part) + g_state
        if part != edges:
            return value
        return jnp.concatenate(
            [
                value[:strip] + halo_ref[at, 0].astype(f32),
                value[strip:-strip],
                value[-strip:] + halo_ref[at, 1].astype(f32),
            ],
            axis=0,
        )

    def backward(step, part, xp_ref, cotangent):
        g_block = jnp.dot(cotangent.astype(bf16), outp_ref[...], preferred_element_type=f32)
        g_block = g_block.astype(bf16)
        put(gblk_ref, part, g_block)
        total = None
        piece = 256
        for start in range(0, wide, piece):
            cut = slice(start, start + piece)
            g_active = lax.dot_general(
                g_block, down_ref[cut, :], ACROSS, preferred_element_type=f32
            )
            slope = take(lambda a, b: slope_ref[step, a * lat_cols : b * lat_cols, cut], part)
            term = lax.dot_general(
                g_active.astype(bf16) * slope, up_ref[:, cut], ACROSS, preferred_element_type=f32
            )
            total = term if total is None else total + term
        g_scaled = total * gain_ref[...]
        normal = take(leading(normal_ref, step), part).astype(f32)
        inverse = take(leading(inverse_ref, step), part)
        inverse = jnp.concatenate([inverse] * (hidden // LANES), axis=1)
        g_mixed = inverse * (g_scaled - mean(g_scaled) - normal * mean(g_scaled * normal))
        put_field(xp_ref, part, g_mixed)

    def leave(part):
        put(cot_ref, part, gathered(part, 3))
        for a, b in part:

            def body(o, carry):
                base = o * lat_cols
                rows = [cot_ref[pl.ds(base + k, runs, stride=BLOCKS), :] for k in range(BLOCKS)]
                turned = jnp.concatenate(rows, axis=0).T
                out_ref[pl.ds(o, channels, stride=lon_rows), :] = turned[:channels]
                return carry

            lax.fori_loop(a, b, body, 0)


    send_state(0)
    obs_start(1)
    conv_inner(xp0_ref, False)
    forward(0, inner, xp0_ref, one_ref, one_ref, xp1_ref)
    arrive_state(0, xp0_ref)
    conv_outer(xp0_ref, False)
    forward(0, edges, xp0_ref, one_ref, one_ref, xp1_ref)
    send_state(1)
    conv_inner(xp1_ref, False)
    forward(1, inner, xp1_ref, one_ref, two_ref, None)
    arrive_state(1, xp1_ref)
    obs_start(0)
    conv_outer(xp1_ref, False)
    forward(1, edges, xp1_ref, one_ref, two_ref, None)
    obs_wait(1)
    observe(1, two_ref, cot_ref)
    backward(1, edges, xp2_ref, take(cells(cot_ref), edges))
    send_landing(2, xp2_ref)
    backward(1, inner, xp2_ref, take(cells(cot_ref), inner))
    conv_own(xp2_ref)
    conv_inner(xp2_ref, True)
    obs_wait(0)
    observe(0, one_ref, pull_ref)
    arrive(2)

    def carried(part):
        value = gathered(part, 2) + take(cells(pull_ref), part)
        put(cot_ref, part, value)
        return value

    backward(0, edges, xp3_ref, carried(edges))
    send_landing(3, xp3_ref)
    backward(0, inner, xp3_ref, carried(inner))
    conv_own(xp3_ref)
    conv_inner(xp3_ref, True)
    leave(inner)
    arrive(3)
    leave(edges)


def shards(
    state_start,
    lift_weight,
    conv_kernel,
    norm_gain,
    up_weight,
    down_weight,
    out_weight,
    obs_cells,
    obs_weights,
    tile_counts,
    obs_owner,
    obs_values,
    obs_precision,
):
    channels, lon_rows, lat_cols = state_start.shape
    hidden, wide = up_weight.shape
    runs = lat_cols // BLOCKS
    count, cap = obs_values.shape[2:4]
    tiles, slot_total = obs_cells.shape[1:3]
    slots = tiles * slot_total
    amount = lon_rows * lat_cols

    vmem = pl.BlockSpec(memory_space=pltpu.VMEM)
    smem = pl.BlockSpec(memory_space=pltpu.SMEM)
    field = (lon_rows + 2 * REACH, runs + 2 * REACH, BLOCKS, hidden)
    result = pl.pallas_call(
        whole_kernel,
        out_shape=jax.ShapeDtypeStruct((channels * lon_rows, lat_cols), f32),
        in_specs=[vmem] * 9 + [smem] + [vmem] * 3,
        out_specs=vmem,
        scratch_shapes=[
            pltpu.VMEM((LANES, LANES), f32),
            pltpu.VMEM((LANES, LANES), f32),
            pltpu.VMEM((LANES, hidden), f32),
            pltpu.VMEM((LANES, hidden), bf16),
            pltpu.VMEM((LANES, hidden), bf16),
            pltpu.VMEM((TAPS * TAPS, BLOCKS, hidden), bf16),
            *[pltpu.VMEM(field, bf16)] * 4,
            *[pltpu.VMEM((amount, LANES), f32)] * 4,
            pltpu.VMEM((lon_rows, runs, BLOCKS, hidden), f32),
            pltpu.VMEM((2, amount, hidden), bf16),
            pltpu.VMEM((2, amount, LANES), f32),
            pltpu.VMEM((2, amount, wide), bf16),
            pltpu.VMEM((amount, hidden), bf16),
            pltpu.VMEM((2 * REACH, runs, BLOCKS, hidden), f32),
            pltpu.VMEM((4, 2, REACH * lat_cols, LANES), bf16),
            pltpu.VMEM((4, 2, REACH * lat_cols, LANES), bf16),
            pltpu.VMEM((2, slots, LANES), f32),
            pltpu.VMEM((2, slots, lon_rows * runs), bf16),
            pltpu.VMEM((2, slots, 2 * LANES), f32),
            *[
                pltpu.VMEM((count, cap, 2 * LANES), bf16),
                pltpu.VMEM((count, cap, LANES), bf16),
            ]
            * 2,
            pltpu.SemaphoreType.DMA((8,)),
            pltpu.SemaphoreType.DMA((8,)),
            pltpu.SemaphoreType.DMA((2, count - 1)),
            pltpu.SemaphoreType.DMA((2, count - 1)),
            pltpu.SemaphoreType.DMA((2,)),
        ],
        compiler_params=pltpu.CompilerParams(
            vmem_limit_bytes=VMEM_LIMIT, collective_id=0, has_side_effects=True
        ),
    )(
        state_start.reshape(channels * lon_rows, lat_cols),
        lift_weight,
        conv_kernel,
        norm_gain.reshape(1, hidden),
        up_weight,
        down_weight,
        out_weight.T,
        obs_cells.transpose(0, 1, 3, 2),
        obs_weights.transpose(0, 1, 3, 2),
        tile_counts,
        obs_owner.transpose(0, 2, 1),
        obs_values[:, 0],
        obs_precision[:, 0],
    )
    return result.reshape(channels, lon_rows, lat_cols)


def solution(mesh):
    placed = (
        P("member", "lon", None),
        P(),
        P(),
        P(),
        P(),
        P(),
        P(),
        P("member", "lon", None, None),
        P("member", "lon", None, None),
        P("member", "lon"),
        P("member", "lon", None),
        P("member", "lon", None, None, None),
        P("member", "lon", None, None, None),
    )
    return jax.shard_map(
        shards, mesh=mesh, in_specs=placed, out_specs=P("member", "lon", None), check_vma=False
    )
```

```python
import jax
import jax.numpy as jnp
from jax import lax
from jax.experimental import pallas as pl
from jax.experimental.pallas import tpu as pltpu
from jax.sharding import PartitionSpec as P

gelu_coef = 0.044715
root_two_pi = 0.7978845608028654
eps_norm = 1e-06
TAPS = 7
REACH = 3
BLOCKS = 8
TILE_LAT = 8
LANES = 128
VMEM_LIMIT = 60 * 1024 * 1024
f32, bf16 = jnp.float32, jnp.bfloat16
ACROSS = (((1,), (1,)), ((), ()))
DOWN = (((0,), (0,)), ((), ()))


def edge_copies(out_ref, in_ref, sems, at):
    send_sem, recv_sem = sems
    count = lax.axis_size("lon")
    here = lax.axis_index("lon")
    ahead, behind = lax.rem(here + 1, count), lax.rem(here + count - 1, count)
    return [
        pltpu.make_async_remote_copy(
            src_ref=out_ref.at[at, side],
            dst_ref=in_ref.at[at, 1 - side],
            send_sem=send_sem.at[2 * at + side],
            recv_sem=recv_sem.at[2 * at + 1 - side],
            device_id={"lon": target},
            device_id_type=pl.DeviceIdType.MESH,
        )
        for side, target in enumerate((behind, ahead))
    ]


def put_ends(xp_ref, at, low, high):
    block = lax.broadcasted_iota(jnp.int32, low.shape, 1)
    runs = xp_ref.shape[1] - 2 * REACH
    before = pltpu.roll(high, 1, 1)
    xp_ref[at, 0:REACH] = jnp.where(block == 0, 0.0, before).astype(bf16)
    after = pltpu.roll(low, BLOCKS - 1, 1)
    xp_ref[at, REACH + runs :] = jnp.where(block == BLOCKS - 1, 0.0, after).astype(bf16)


def put_tiles(xp_ref, row, values):
    runs = values.shape[0] // BLOCKS
    tiles = values.reshape(runs, BLOCKS, values.shape[1])
    xp_ref[row + REACH, REACH : REACH + runs] = tiles.astype(bf16)
    put_ends(xp_ref, row + REACH, tiles[:REACH], tiles[runs - REACH :])


def tree(terms):
    while len(terms) > 1:
        terms = [
            terms[k] + terms[k + 1] if k + 1 < len(terms) else terms[k]
            for k in range(0, len(terms), 2)
        ]
    return terms[0]


def conv_row(xp_ref, kb_ref, mix_ref, o, to, flip, taps=range(TAPS)):
    runs = mix_ref.shape[1]
    last = TAPS * TAPS - 1
    for first in range(0, len(taps), 3):
        lines = taps[first : first + 3]
        weights = {}
        for i in lines:
            for j in range(TAPS):
                tap = i * TAPS + j
                weights[i, j] = kb_ref[last - tap if flip else tap]
        window = {i: [xp_ref[o + i, q] for q in range(TAPS - 1)] for i in lines}
        for r in range(runs):
            sums = []
            for i in lines:
                window[i].append(xp_ref[o + i, r + TAPS - 1])
                sums.append(tree([weights[i, j] * window[i][j] for j in range(TAPS)]))
                window[i].pop(0)
            term = tree(sums).astype(f32)
            mix_ref[to, r] = term if first == 0 else mix_ref[to, r] + term


def whole_kernel(
    state_ref,
    lift_ref,
    kern_ref,
    gain_ref,
    up_hbm,
    down_hbm,
    outw_ref,
    cell_ref,
    wts_ref,
    limit_ref,
    owner_ref,
    vals_hbm,
    prec_hbm,
    out_ref,
    up_ref,
    down_ref,
    vals_ref,
    prec_ref,
    tin_ref,
    nat_ref,
    pad_ref,
    liftp_ref,
    outp_ref,
    kb_ref,
    xp0_ref,
    xp1_ref,
    xp2_ref,
    xp3_ref,
    one_ref,
    two_ref,
    cot_ref,
    pull_ref,
    mix_ref,
    normal_ref,
    inverse_ref,
    slope_ref,
    gblk_ref,
    mid_ref,
    land_ref,
    edge_ref,
    halo_ref,
    code_ref,
    op_ref,
    chosen_ref,
    late_ref,
    early_ref,
    late_in_ref,
    early_in_ref,
    send_sem,
    recv_sem,
    obs_send,
    obs_recv,
    own_sem,
    load_sem,
):
    count = lax.axis_size("lon")
    here = lax.axis_index("lon")
    lon_rows, runs, _, hidden = mix_ref.shape
    lat_cols = runs * BLOCKS
    wide = up_ref.shape[1]
    channels = vals_ref.shape[-1]
    cap = vals_ref.shape[2]
    tiles, points, each = cell_ref.shape[1:]
    slots = tiles * each
    sems = (send_sem, recv_sem)
    quarter = lon_rows // 4
    inner = ((quarter, lon_rows - quarter),)
    edges = ((0, quarter), (lon_rows - quarter, lon_rows))
    barrier = pltpu.get_barrier_semaphore()
    ones = jnp.full((hidden, LANES), 1.0 / hidden, bf16)

    def peer(step):
        return lax.rem(here + step, count)

    def greet(step, carry):
        pl.semaphore_signal(
            barrier, inc=1, device_id={"lon": peer(step)}, device_id_type=pl.DeviceIdType.MESH
        )
        return carry

    lax.fori_loop(1, count, greet, 0)
    loads = [
        pltpu.make_async_copy(source, target, load_sem.at[k])
        for k, (source, target) in enumerate(
            (
                (vals_hbm, vals_ref),
                (prec_hbm, prec_ref),
                (up_hbm, up_ref),
                (down_hbm, down_ref),
            )
        )
    ]
    for load in loads:
        load.start()


    for ref, into_ref in ((lift_ref, liftp_ref), (outw_ref, outp_ref)):
        pad_ref[...] = jnp.zeros_like(pad_ref)
        pad_ref[0:channels, :] = ref[...].astype(f32)
        into_ref[...] = pad_ref[...].astype(bf16)

    tin_ref[...] = jnp.zeros_like(tin_ref)

    def tap_row(tap, carry):
        row = kern_ref[pl.ds(tap, 1), :]
        kb_ref[tap] = jnp.broadcast_to(row, (BLOCKS, hidden)).astype(bf16)
        return carry

    lax.fori_loop(0, TAPS * TAPS, tap_row, 0)

    def enter(o, carry):
        tin_ref[0:channels, :] = state_ref[pl.ds(o, channels, stride=lon_rows), :]
        nat_ref[...] = tin_ref[...].T
        base = pl.multiple_of(o * lat_cols, lat_cols)
        cells = jnp.concatenate(
            [nat_ref[pl.ds(r, BLOCKS, stride=runs), :] for r in range(runs)], axis=0
        )
        one_ref[pl.ds(base, lat_cols), :] = cells
        lifted = jnp.dot(cells.astype(bf16), liftp_ref[...], preferred_element_type=f32)
        put_tiles(xp0_ref, o, lifted)
        return carry

    lax.fori_loop(0, lon_rows, enter, 0)


    for load in loads:
        load.wait()

    free = LANES - channels
    turns = [(channels - (channels - free * (2 - k))) % LANES for k in range(2)] + [channels]

    def obs_row(band, carry):
        filled = lambda part: jnp.concatenate(
            [part, jnp.zeros((cap, LANES - channels), f32)], axis=1
        )
        spare = filled(prec_ref[0, band])
        lane = lax.broadcasted_iota(jnp.int32, (cap, LANES), 1)
        for place, part in enumerate((vals_ref[1, band], prec_ref[1, band], vals_ref[0, band])):
            moved = pltpu.roll(spare, turns[place], 1)
            both = jnp.where(lane < channels, filled(part), moved)
            if place < 2:
                late_ref[band, :, place * LANES : (place + 1) * LANES] = both.astype(bf16)
            else:
                early_ref[band] = both.astype(bf16)
        return carry

    lax.fori_loop(0, count, obs_row, 0)


    def lookup(moment):
        owner = owner_ref[moment]
        column = jnp.broadcast_to(owner.astype(f32), (LANES, slots)).T
        pieces = []
        for part in range(slots // LANES):
            row = owner[:, part * LANES : (part + 1) * LANES]
            earlier = lax.broadcasted_iota(jnp.int32, (slots, LANES), 0)
            later = lax.broadcasted_iota(jnp.int32, (slots, LANES), 1) + part * LANES
            same = (column == row.astype(f32)) & (earlier < later)
            place = jnp.sum(jnp.where(same, 1.0, 0.0), axis=0, keepdims=True)
            lane = lax.broadcasted_iota(jnp.int32, (1, LANES), 1)
            limit = jnp.zeros((1, LANES), jnp.int32)
            for k in range(LANES // each):
                tile = part * (LANES // each) + k
                limit = jnp.where(lane >= k * each, limit_ref[moment, tile] + k * each, limit)
            code = row.astype(f32) * cap + place
            pieces.append(jnp.where(lane < limit, code, -1.0))
        code = jnp.concatenate(pieces, axis=1)
        code_ref[moment] = jnp.broadcast_to(code, (LANES, slots)).T

    lookup(0)
    lookup(1)

    pl.semaphore_wait(barrier, count - 1)

    strip = REACH * lat_cols
    total_rows = lon_rows * lat_cols

    def send(at, west, east):
        edge_ref[at, 0] = west.astype(bf16)
        edge_ref[at, 1] = east.astype(bf16)
        for copy in edge_copies(edge_ref, halo_ref, sems, at):
            copy.start()

    def send_state(at):
        send(at, one_ref[0:strip, :], one_ref[total_rows - strip :, :])

    def arrive(at):
        for copy in edge_copies(edge_ref, halo_ref, sems, at):
            copy.wait()

    def arrive_state(at, xp_ref):
        arrive(at)
        for side, first in enumerate((-REACH, lon_rows)):
            lifted = jnp.dot(halo_ref[at, side], liftp_ref[...], preferred_element_type=f32)
            for k in range(REACH):
                put_tiles(xp_ref, first + k, lifted[k * lat_cols : (k + 1) * lat_cols])

    boxes = ((early_ref, early_in_ref), (late_ref, late_in_ref))

    def obs_copy(moment, step, band):
        out_box, in_box = boxes[moment]
        return pltpu.make_async_remote_copy(
            src_ref=out_box.at[band],
            dst_ref=in_box.at[here],
            send_sem=obs_send.at[moment, step - 1],
            recv_sem=obs_recv.at[moment, step - 1],
            device_id={"lon": peer(step)},
            device_id_type=pl.DeviceIdType.MESH,
        )

    def own_copy(moment):
        out_box, in_box = boxes[moment]
        return pltpu.make_async_copy(out_box.at[here], in_box.at[here], own_sem.at[moment])

    def obs_start(moment):
        def start(step, carry):
            obs_copy(moment, step, peer(step)).start()
            return carry

        lax.fori_loop(1, count, start, 0)
        own_copy(moment).start()

    def obs_wait(moment):
        def wait(step, carry):
            obs_copy(moment, step, peer(step)).wait_send()
            source = peer(count - step)
            out_box, in_box = boxes[moment]
            pltpu.make_async_remote_copy(
                src_ref=out_box.at[source],
                dst_ref=in_box.at[source],
                send_sem=obs_send.at[moment, step - 1],
                recv_sem=obs_recv.at[moment, step - 1],
                device_id={"lon": peer(step)},
                device_id_type=pl.DeviceIdType.MESH,
            ).wait_recv()
            return carry

        lax.fori_loop(1, count, wait, 0)
        own_copy(moment).wait()


    def take(load, part):
        chunks = [load(a, b) for a, b in part]
        return chunks[0] if len(chunks) == 1 else jnp.concatenate(chunks, axis=0)

    def cells(ref):
        return lambda a, b: ref[a * lat_cols : b * lat_cols, :]

    def leading(ref, step):
        return lambda a, b: ref[step, a * lat_cols : b * lat_cols, :]

    def put(ref, part, values, step=None):
        at = 0
        for a, b in part:
            size = (b - a) * lat_cols
            where = slice(a * lat_cols, b * lat_cols)
            if step is None:
                ref[where, :] = values[at : at + size]
            else:
                ref[step, where, :] = values[at : at + size]
            at += size

    def put_field(xp_ref, part, values):
        at = 0
        for a, b in part:
            for o in range(a, b):
                put_tiles(xp_ref, o, values[at : at + lat_cols])
                at += lat_cols

    def sums(part):
        return take(
            lambda a, b: mix_ref[a:b].reshape((b - a) * lat_cols, hidden),
            part,
        )

    def mean(values):
        wide_mean = jnp.dot(values.astype(bf16), ones, preferred_element_type=f32)
        return jnp.concatenate([wide_mean] * (hidden // LANES), axis=1)

    def conv_inner(xp_ref, flip):
        def body(o, carry):
            conv_row(xp_ref, kb_ref, mix_ref, o, o, flip)
            return carry

        lax.fori_loop(REACH, lon_rows - REACH, body, 0)

    def conv_outer(xp_ref, flip):
        def body(k, carry):
            o = jnp.where(k < REACH, k, lon_rows - 2 * REACH + k)
            conv_row(xp_ref, kb_ref, mix_ref, o, o, flip)
            return carry

        lax.fori_loop(0, 2 * REACH, body, 0)

    def conv_own(xp_ref):
        for k in range(REACH):
            conv_row(xp_ref, kb_ref, mix_ref, k, k, True, range(REACH - k, TAPS))
            o = lon_rows - 1 - k
            conv_row(xp_ref, kb_ref, mix_ref, o, o, True, range(0, TAPS - REACH + k))

    def send_landing(at, xp_ref):
        for k in range(REACH):
            conv_row(xp_ref, kb_ref, land_ref, k - REACH, k, True, range(2 * REACH - k, TAPS))
            conv_row(xp_ref, kb_ref, land_ref, lon_rows + k, REACH + k, True, range(0, REACH - k))
        landed = land_ref[...].reshape(2 * strip, hidden).astype(bf16)
        g_state = lax.dot_general(landed, liftp_ref[...], ACROSS, preferred_element_type=f32)
        send(at, g_state[:strip], g_state[strip:])

    def forward(step, part, xp_ref, source_ref, target_ref, next_ref):
        mixed = sums(part)
        center = mixed - mean(mixed)
        inverse = lax.rsqrt(mean(center * center) + eps_norm)
        normal = center * inverse
        put(normal_ref, part, normal.astype(bf16), step)
        put(inverse_ref, part, inverse[:, :LANES], step)
        normed = (normal * gain_ref[...]).astype(bf16)
        total = take(
            lambda a, b: xp_ref[a + REACH : b + REACH, REACH : REACH + runs]
            .reshape((b - a) * lat_cols, hidden)
            .astype(f32),
            part,
        )
        piece = 256
        one = bf16(root_two_pi)
        three = bf16(root_two_pi * gelu_coef)
        half_one = bf16(0.5)
        for start in range(0, wide, piece):
            cut = slice(start, start + piece)
            z = jnp.dot(normed, up_ref[:, cut], preferred_element_type=f32).astype(bf16)
            square = z * z
            tanh_val = jnp.tanh(z * (one + three * square))
            share = half_one + half_one * tanh_val
            active = z * share
            rest = bf16(1.0) - share
            bend = z * (bf16(2.0) * one + bf16(6.0) * three * square)
            slope = share + share * (rest * bend)
            at = 0
            for a, b in part:
                size = (b - a) * lat_cols
                slope_ref[step, a * lat_cols : b * lat_cols, cut] = slope[at : at + size]
                at += size
            total = total + jnp.dot(active, down_ref[cut, :], preferred_element_type=f32)
        change = lax.dot_general(
            total.astype(bf16), outp_ref[...], ACROSS, preferred_element_type=f32
        )
        state = take(cells(source_ref), part) + change
        put(target_ref, part, state)
        if next_ref is not None:
            lifted = jnp.dot(state.astype(bf16), liftp_ref[...], preferred_element_type=f32)
            put_field(next_ref, part, lifted)

    def observe(moment, state_ref, target_ref):
        spots = lon_rows * runs
        by_point = lambda ref: jnp.concatenate([ref[moment, g] for g in range(tiles)], axis=1)
        cell = by_point(cell_ref)
        lane = lax.broadcasted_iota(jnp.int32, (points, slots), 1)
        first = ((lane // each) * TILE_LAT) % runs
        spot = (cell // TILE_LAT) * runs + first + cell % TILE_LAT
        weight = by_point(wts_ref)
        number = lax.broadcasted_iota(jnp.int32, (spots, slots), 0)
        lines = jnp.zeros((spots, slots), f32)
        for p in range(points):
            hit = spot[p : p + 1, :] == number
            lines = jnp.where(hit, lines + weight[p : p + 1, :], lines)
        op_ref[moment] = lines.T.astype(bf16)
        places = count * cap
        code = code_ref[moment]
        line = lax.broadcasted_iota(jnp.int32, (slots, LANES), 1).astype(f32)
        select = jnp.concatenate(
            [
                jnp.where(code - float(start) == line, 1.0, 0.0).astype(bf16)
                for start in range(0, places, LANES)
            ],
            axis=1,
        )
        data = late_in_ref[...].reshape(places, 2 * LANES)
        chosen = jnp.dot(select, data, preferred_element_type=f32)
        if moment == 0:
            data = early_in_ref[...].reshape(places, LANES)
            third = jnp.dot(select, data, preferred_element_type=f32)
            tiles3 = (chosen[:, :LANES], chosen[:, LANES:], third)
            back = [pltpu.roll(t, (LANES - n) % LANES, 1) for t, n in zip(tiles3, turns)]
            lane = lax.broadcasted_iota(jnp.int32, (slots, LANES), 1)
            start = channels - 2 * free
            weights = jnp.where(
                lane < start, back[2], jnp.where(lane < start + free, back[0], back[1])
            )
            weights = jnp.where(lane < channels, weights, 0.0)
            chosen = jnp.concatenate([third, weights], axis=1)
        chosen_ref[moment] = chosen
        size = slots // BLOCKS
        for block in range(BLOCKS):
            at = pl.ds(block, spots, stride=BLOCKS)
            mine = slice(block * size, (block + 1) * size)
            op = op_ref[moment, mine, :]
            equiv = jnp.dot(op, state_ref[at, :].astype(bf16), preferred_element_type=f32)
            chosen = chosen_ref[moment, mine, :]
            misfit = chosen[:, LANES:] * (equiv - chosen[:, :LANES])
            lane = lax.broadcasted_iota(jnp.int32, (size, LANES), 1)
            misfit = jnp.where(lane < channels, misfit, 0.0)
            target_ref[at, :] = lax.dot_general(
                op, misfit.astype(bf16), DOWN, preferred_element_type=f32
            )

    def gathered(part, at):
        g_lifted = (take(cells(gblk_ref), part).astype(f32) + sums(part)).astype(bf16)
        g_state = lax.dot_general(g_lifted, liftp_ref[...], ACROSS, preferred_element_type=f32)
        value = take(cells(cot_ref), part) + g_state
        if part != edges:
            return value
        return jnp.concatenate(
            [
                value[:strip] + halo_ref[at, 0].astype(f32),
                value[strip:-strip],
                value[-strip:] + halo_ref[at, 1].astype(f32),
            ],
            axis=0,
        )

    def backward(step, part, xp_ref, cotangent):
        g_block = jnp.dot(cotangent.astype(bf16), outp_ref[...], preferred_element_type=f32)
        g_block = g_block.astype(bf16)
        put(gblk_ref, part, g_block)
        piece = 256
        for start in range(0, wide, piece):
            cut = slice(start, start + piece)
            g_active = lax.dot_general(
                g_block, down_ref[cut, :], ACROSS, preferred_element_type=f32
            )
            slope = take(lambda a, b: slope_ref[step, a * lat_cols : b * lat_cols, cut], part)
            mid_ref[:, cut] = g_active.astype(bf16) * slope
        total = lax.dot_general(mid_ref[...], up_ref[...], ACROSS, preferred_element_type=f32)
        g_scaled = total * gain_ref[...]
        normal = take(leading(normal_ref, step), part).astype(f32)
        inverse = take(leading(inverse_ref, step), part)
        inverse = jnp.concatenate([inverse] * (hidden // LANES), axis=1)
        g_mixed = inverse * (g_scaled - mean(g_scaled) - normal * mean(g_scaled * normal))
        put_field(xp_ref, part, g_mixed)

    def leave(part):
        put(out_ref, part, gathered(part, 3))


    send_state(0)
    obs_start(1)
    conv_inner(xp0_ref, False)
    forward(0, inner, xp0_ref, one_ref, one_ref, xp1_ref)
    arrive_state(0, xp0_ref)
    conv_outer(xp0_ref, False)
    forward(0, edges, xp0_ref, one_ref, one_ref, xp1_ref)
    send_state(1)
    conv_inner(xp1_ref, False)
    forward(1, inner, xp1_ref, one_ref, two_ref, None)
    arrive_state(1, xp1_ref)
    obs_start(0)
    conv_outer(xp1_ref, False)
    forward(1, edges, xp1_ref, one_ref, two_ref, None)
    obs_wait(1)
    observe(1, two_ref, cot_ref)
    backward(1, edges, xp2_ref, take(cells(cot_ref), edges))
    send_landing(2, xp2_ref)
    obs_wait(0)
    observe(0, one_ref, pull_ref)
    backward(1, inner, xp2_ref, take(cells(cot_ref), inner))
    conv_own(xp2_ref)
    conv_inner(xp2_ref, True)
    arrive(2)

    def carried(part):
        value = gathered(part, 2) + take(cells(pull_ref), part)
        put(cot_ref, part, value)
        return value

    backward(0, edges, xp3_ref, carried(edges))
    send_landing(3, xp3_ref)
    backward(0, inner, xp3_ref, carried(inner))
    conv_own(xp3_ref)
    conv_inner(xp3_ref, True)
    leave(inner)
    arrive(3)
    leave(edges)


def turn_kernel(cells_hbm, out_ref, cells_ref, sem):
    lat_cols = out_ref.shape[1]
    lon_rows = cells_ref.shape[0] // lat_cols
    channels = out_ref.shape[0] // lon_rows
    runs = lat_cols // BLOCKS
    parts = sem.shape[0]
    size = lon_rows // parts
    loads = []
    for k in range(parts):
        at = pl.ds(k * size * lat_cols, size * lat_cols)
        load = pltpu.make_async_copy(cells_hbm.at[at], cells_ref.at[at], sem.at[k])
        load.start()
        loads.append(load)

    def body(o, carry):
        base = o * lat_cols
        rows = [cells_ref[pl.ds(base + k, runs, stride=BLOCKS), :] for k in range(BLOCKS)]
        turned = jnp.concatenate(rows, axis=0).T
        out_ref[pl.ds(o, channels, stride=lon_rows), :] = turned[:channels]
        return carry

    for k, load in enumerate(loads):
        load.wait()
        lax.fori_loop(k * size, (k + 1) * size, body, 0, unroll=2)


def shards(
    state_start,
    lift_weight,
    conv_kernel,
    norm_gain,
    up_weight,
    down_weight,
    out_weight,
    obs_cells,
    obs_weights,
    tile_counts,
    obs_owner,
    obs_values,
    obs_precision,
):
    channels, lon_rows, lat_cols = state_start.shape
    hidden, wide = up_weight.shape
    runs = lat_cols // BLOCKS
    count, cap = obs_values.shape[2:4]
    tiles, slot_total = obs_cells.shape[1:3]
    slots = tiles * slot_total
    amount = lon_rows * lat_cols

    vmem = pl.BlockSpec(memory_space=pltpu.VMEM)
    smem = pl.BlockSpec(memory_space=pltpu.SMEM)
    hbm = pl.BlockSpec(memory_space=pl.ANY)
    field = (lon_rows + 2 * REACH, runs + 2 * REACH, BLOCKS, hidden)
    result = pl.pallas_call(
        whole_kernel,
        out_shape=jax.ShapeDtypeStruct((amount, LANES), f32),
        in_specs=[vmem] * 4 + [hbm] * 2 + [vmem] * 3 + [smem, vmem] + [hbm] * 2,
        out_specs=vmem,
        scratch_shapes=[
            pltpu.VMEM((hidden, wide), bf16),
            pltpu.VMEM((wide, hidden), bf16),
            *[pltpu.VMEM((2, count, cap, channels), f32)] * 2,
            pltpu.VMEM((LANES, LANES), f32),
            pltpu.VMEM((LANES, LANES), f32),
            pltpu.VMEM((LANES, hidden), f32),
            pltpu.VMEM((LANES, hidden), bf16),
            pltpu.VMEM((LANES, hidden), bf16),
            pltpu.VMEM((TAPS * TAPS, BLOCKS, hidden), bf16),
            *[pltpu.VMEM(field, bf16)] * 4,
            *[pltpu.VMEM((amount, LANES), f32)] * 4,
            pltpu.VMEM((lon_rows, runs, BLOCKS, hidden), f32),
            pltpu.VMEM((2, amount, hidden), bf16),
            pltpu.VMEM((2, amount, LANES), f32),
            pltpu.VMEM((2, amount, wide), bf16),
            pltpu.VMEM((amount, hidden), bf16),
            pltpu.VMEM((amount // 2, wide), bf16),
            pltpu.VMEM((2 * REACH, runs, BLOCKS, hidden), f32),
            pltpu.VMEM((4, 2, REACH * lat_cols, LANES), bf16),
            pltpu.VMEM((4, 2, REACH * lat_cols, LANES), bf16),
            pltpu.VMEM((2, slots, LANES), f32),
            pltpu.VMEM((2, slots, lon_rows * runs), bf16),
            pltpu.VMEM((2, slots, 2 * LANES), f32),
            *[
                pltpu.VMEM((count, cap, 2 * LANES), bf16),
                pltpu.VMEM((count, cap, LANES), bf16),
            ]
            * 2,
            pltpu.SemaphoreType.DMA((8,)),
            pltpu.SemaphoreType.DMA((8,)),
            pltpu.SemaphoreType.DMA((2, count - 1)),
            pltpu.SemaphoreType.DMA((2, count - 1)),
            pltpu.SemaphoreType.DMA((2,)),
            pltpu.SemaphoreType.DMA((4,)),
        ],
        compiler_params=pltpu.CompilerParams(
            vmem_limit_bytes=VMEM_LIMIT, collective_id=0, has_side_effects=True
        ),
    )(
        state_start.reshape(channels * lon_rows, lat_cols),
        lift_weight,
        conv_kernel,
        norm_gain.reshape(1, hidden),
        up_weight,
        down_weight,
        out_weight.T,
        obs_cells.transpose(0, 1, 3, 2),
        obs_weights.transpose(0, 1, 3, 2),
        tile_counts,
        obs_owner.transpose(0, 2, 1),
        obs_values[:, 0],
        obs_precision[:, 0],
    )
    turned = pl.pallas_call(
        turn_kernel,
        out_shape=jax.ShapeDtypeStruct((channels * lon_rows, lat_cols), f32),
        in_specs=[hbm],
        out_specs=vmem,
        scratch_shapes=[pltpu.VMEM((amount, LANES), f32), pltpu.SemaphoreType.DMA((4,))],
        compiler_params=pltpu.CompilerParams(vmem_limit_bytes=VMEM_LIMIT),
    )(result)
    return turned.reshape(channels, lon_rows, lat_cols)


def solution(mesh):
    placed = (
        P("member", "lon", None),
        P(),
        P(),
        P(),
        P(),
        P(),
        P(),
        P("member", "lon", None, None),
        P("member", "lon", None, None),
        P("member", "lon"),
        P("member", "lon", None),
        P("member", "lon", None, None, None),
        P("member", "lon", None, None, None),
    )
    return jax.shard_map(
        shards, mesh=mesh, in_specs=placed, out_specs=P("member", "lon", None), check_vma=False
    )
```

```python
import jax
import jax.numpy as jnp
from jax import lax
from jax.experimental import pallas as pl
from jax.experimental.pallas import tpu as pltpu
from jax.sharding import PartitionSpec as P

gelu_coef = 0.044715
root_two_pi = 0.7978845608028654
eps_norm = 1e-06
TAPS = 7
REACH = 3
BLOCKS = 8
TILE_LAT = 8
LANES = 128
VMEM_LIMIT = 60 * 1024 * 1024
f32, bf16 = jnp.float32, jnp.bfloat16
ACROSS = (((1,), (1,)), ((), ()))
DOWN = (((0,), (0,)), ((), ()))


def edge_copies(out_ref, in_ref, sems, at):
    send_sem, recv_sem = sems
    count = lax.axis_size("lon")
    here = lax.axis_index("lon")
    ahead, behind = lax.rem(here + 1, count), lax.rem(here + count - 1, count)
    return [
        pltpu.make_async_remote_copy(
            src_ref=out_ref.at[at, side],
            dst_ref=in_ref.at[at, 1 - side],
            send_sem=send_sem.at[2 * at + side],
            recv_sem=recv_sem.at[2 * at + 1 - side],
            device_id={"lon": target},
            device_id_type=pl.DeviceIdType.MESH,
        )
        for side, target in enumerate((behind, ahead))
    ]


def put_ends(xp_ref, at, low, high):
    block = lax.broadcasted_iota(jnp.int32, low.shape, 1)
    runs = xp_ref.shape[1] - 2 * REACH
    before = pltpu.roll(high, 1, 1)
    xp_ref[at, 0:REACH] = jnp.where(block == 0, 0.0, before).astype(bf16)
    after = pltpu.roll(low, BLOCKS - 1, 1)
    xp_ref[at, REACH + runs :] = jnp.where(block == BLOCKS - 1, 0.0, after).astype(bf16)


def put_tiles(xp_ref, row, values):
    runs = values.shape[0] // BLOCKS
    tiles = values.reshape(runs, BLOCKS, values.shape[1])
    xp_ref[row + REACH, REACH : REACH + runs] = tiles.astype(bf16)
    put_ends(xp_ref, row + REACH, tiles[:REACH], tiles[runs - REACH :])


def tree(terms):
    while len(terms) > 1:
        terms = [
            terms[k] + terms[k + 1] if k + 1 < len(terms) else terms[k]
            for k in range(0, len(terms), 2)
        ]
    return terms[0]


def conv_row(xp_ref, kb_ref, mix_ref, o, to, flip, taps=range(TAPS)):
    runs = mix_ref.shape[1]
    last = TAPS * TAPS - 1
    for first in range(0, len(taps), 3):
        lines = taps[first : first + 3]
        weights = {}
        for i in lines:
            for j in range(TAPS):
                tap = i * TAPS + j
                weights[i, j] = kb_ref[last - tap if flip else tap]
        window = {i: [xp_ref[o + i, q] for q in range(TAPS - 1)] for i in lines}
        for r in range(runs):
            sums = []
            for i in lines:
                window[i].append(xp_ref[o + i, r + TAPS - 1])
                sums.append(tree([weights[i, j] * window[i][j] for j in range(TAPS)]))
                window[i].pop(0)
            term = tree(sums).astype(f32)
            mix_ref[to, r] = term if first == 0 else mix_ref[to, r] + term


def whole_kernel(
    state_ref,
    lift_ref,
    kern_ref,
    gain_ref,
    up_hbm,
    down_hbm,
    outw_ref,
    cell_ref,
    wts_ref,
    limit_ref,
    owner_ref,
    vals_hbm,
    prec_hbm,
    out_ref,
    up_ref,
    down_ref,
    vals_ref,
    prec_ref,
    tin_ref,
    nat_ref,
    pad_ref,
    liftp_ref,
    outp_ref,
    kb_ref,
    xp0_ref,
    xp1_ref,
    xp2_ref,
    xp3_ref,
    one_ref,
    two_ref,
    cot_ref,
    pull_ref,
    mix_ref,
    normal_ref,
    inverse_ref,
    slope_ref,
    gblk_ref,
    mid_ref,
    land_ref,
    edge_ref,
    halo_ref,
    code_ref,
    op_ref,
    chosen_ref,
    late_ref,
    early_ref,
    late_in_ref,
    early_in_ref,
    send_sem,
    recv_sem,
    obs_send,
    obs_recv,
    own_sem,
    load_sem,
):
    count = lax.axis_size("lon")
    here = lax.axis_index("lon")
    lon_rows, runs, _, hidden = mix_ref.shape
    lat_cols = runs * BLOCKS
    wide = up_ref.shape[1]
    channels = vals_ref.shape[-1]
    cap = vals_ref.shape[2]
    tiles, points, each = cell_ref.shape[1:]
    slots = tiles * each
    sems = (send_sem, recv_sem)
    quarter = lon_rows // 4
    inner = ((quarter, lon_rows - quarter),)
    edges = ((0, quarter), (lon_rows - quarter, lon_rows))
    barrier = pltpu.get_barrier_semaphore()
    ones = jnp.full((hidden, LANES), 1.0 / hidden, bf16)

    def peer(step):
        return lax.rem(here + step, count)

    def greet(step, carry):
        pl.semaphore_signal(
            barrier, inc=1, device_id={"lon": peer(step)}, device_id_type=pl.DeviceIdType.MESH
        )
        return carry

    lax.fori_loop(1, count, greet, 0)
    loads = [
        pltpu.make_async_copy(source, target, load_sem.at[k])
        for k, (source, target) in enumerate(
            (
                (vals_hbm, vals_ref),
                (prec_hbm, prec_ref),
                (up_hbm, up_ref),
                (down_hbm, down_ref),
            )
        )
    ]
    for load in loads:
        load.start()


    for ref, into_ref in ((lift_ref, liftp_ref), (outw_ref, outp_ref)):
        pad_ref[...] = jnp.zeros_like(pad_ref)
        pad_ref[0:channels, :] = ref[...].astype(f32)
        into_ref[...] = pad_ref[...].astype(bf16)

    tin_ref[...] = jnp.zeros_like(tin_ref)

    def tap_row(tap, carry):
        row = kern_ref[pl.ds(tap, 1), :]
        kb_ref[tap] = jnp.broadcast_to(row, (BLOCKS, hidden)).astype(bf16)
        return carry

    lax.fori_loop(0, TAPS * TAPS, tap_row, 0)

    def enter(o, carry):
        tin_ref[0:channels, :] = state_ref[pl.ds(o, channels, stride=lon_rows), :]
        nat_ref[...] = tin_ref[...].T
        base = pl.multiple_of(o * lat_cols, lat_cols)
        cells = jnp.concatenate(
            [nat_ref[pl.ds(r, BLOCKS, stride=runs), :] for r in range(runs)], axis=0
        )
        one_ref[pl.ds(base, lat_cols), :] = cells
        lifted = jnp.dot(cells.astype(bf16), liftp_ref[...], preferred_element_type=f32)
        put_tiles(xp0_ref, o, lifted)
        return carry

    lax.fori_loop(0, lon_rows, enter, 0)


    for load in loads:
        load.wait()

    free = LANES - channels
    turns = [(channels - (channels - free * (2 - k))) % LANES for k in range(2)] + [channels]

    def obs_row(band, carry):
        filled = lambda part: jnp.concatenate(
            [part, jnp.zeros((cap, LANES - channels), f32)], axis=1
        )
        spare = filled(prec_ref[0, band])
        lane = lax.broadcasted_iota(jnp.int32, (cap, LANES), 1)
        for place, part in enumerate((vals_ref[1, band], prec_ref[1, band], vals_ref[0, band])):
            moved = pltpu.roll(spare, turns[place], 1)
            both = jnp.where(lane < channels, filled(part), moved)
            if place < 2:
                late_ref[band, :, place * LANES : (place + 1) * LANES] = both.astype(bf16)
            else:
                early_ref[band] = both.astype(bf16)
        return carry

    lax.fori_loop(0, count, obs_row, 0)


    def lookup(moment):
        owner = owner_ref[moment]
        column = jnp.broadcast_to(owner.astype(f32), (LANES, slots)).T
        pieces = []
        for part in range(slots // LANES):
            row = owner[:, part * LANES : (part + 1) * LANES]
            earlier = lax.broadcasted_iota(jnp.int32, (slots, LANES), 0)
            later = lax.broadcasted_iota(jnp.int32, (slots, LANES), 1) + part * LANES
            same = (column == row.astype(f32)) & (earlier < later)
            place = jnp.sum(jnp.where(same, 1.0, 0.0), axis=0, keepdims=True)
            lane = lax.broadcasted_iota(jnp.int32, (1, LANES), 1)
            limit = jnp.zeros((1, LANES), jnp.int32)
            for k in range(LANES // each):
                tile = part * (LANES // each) + k
                limit = jnp.where(lane >= k * each, limit_ref[moment, tile] + k * each, limit)
            code = row.astype(f32) * cap + place
            pieces.append(jnp.where(lane < limit, code, -1.0))
        code = jnp.concatenate(pieces, axis=1)
        code_ref[moment] = jnp.broadcast_to(code, (LANES, slots)).T

    lookup(0)
    lookup(1)

    pl.semaphore_wait(barrier, count - 1)

    strip = REACH * lat_cols
    total_rows = lon_rows * lat_cols

    def send(at, west, east):
        edge_ref[at, 0] = west.astype(bf16)
        edge_ref[at, 1] = east.astype(bf16)
        for copy in edge_copies(edge_ref, halo_ref, sems, at):
            copy.start()

    def send_state(at):
        send(at, one_ref[0:strip, :], one_ref[total_rows - strip :, :])

    def arrive(at):
        for copy in edge_copies(edge_ref, halo_ref, sems, at):
            copy.wait()

    def arrive_state(at, xp_ref):
        arrive(at)
        for side, first in enumerate((-REACH, lon_rows)):
            lifted = jnp.dot(halo_ref[at, side], liftp_ref[...], preferred_element_type=f32)
            for k in range(REACH):
                put_tiles(xp_ref, first + k, lifted[k * lat_cols : (k + 1) * lat_cols])

    boxes = ((early_ref, early_in_ref), (late_ref, late_in_ref))

    def obs_copy(moment, step, band):
        out_box, in_box = boxes[moment]
        return pltpu.make_async_remote_copy(
            src_ref=out_box.at[band],
            dst_ref=in_box.at[here],
            send_sem=obs_send.at[moment, step - 1],
            recv_sem=obs_recv.at[moment, step - 1],
            device_id={"lon": peer(step)},
            device_id_type=pl.DeviceIdType.MESH,
        )

    def own_copy(moment):
        out_box, in_box = boxes[moment]
        return pltpu.make_async_copy(out_box.at[here], in_box.at[here], own_sem.at[moment])

    def obs_start(moment):
        def start(step, carry):
            obs_copy(moment, step, peer(step)).start()
            return carry

        lax.fori_loop(1, count, start, 0)
        own_copy(moment).start()

    def obs_wait(moment):
        def wait(step, carry):
            obs_copy(moment, step, peer(step)).wait_send()
            source = peer(count - step)
            out_box, in_box = boxes[moment]
            pltpu.make_async_remote_copy(
                src_ref=out_box.at[source],
                dst_ref=in_box.at[source],
                send_sem=obs_send.at[moment, step - 1],
                recv_sem=obs_recv.at[moment, step - 1],
                device_id={"lon": peer(step)},
                device_id_type=pl.DeviceIdType.MESH,
            ).wait_recv()
            return carry

        lax.fori_loop(1, count, wait, 0)
        own_copy(moment).wait()


    def take(load, part):
        chunks = [load(a, b) for a, b in part]
        return chunks[0] if len(chunks) == 1 else jnp.concatenate(chunks, axis=0)

    def cells(ref):
        return lambda a, b: ref[a * lat_cols : b * lat_cols, :]

    def leading(ref, step):
        return lambda a, b: ref[step, a * lat_cols : b * lat_cols, :]

    def put(ref, part, values, step=None):
        at = 0
        for a, b in part:
            size = (b - a) * lat_cols
            where = slice(a * lat_cols, b * lat_cols)
            if step is None:
                ref[where, :] = values[at : at + size]
            else:
                ref[step, where, :] = values[at : at + size]
            at += size

    def put_field(xp_ref, part, values):
        at = 0
        for a, b in part:
            for o in range(a, b):
                put_tiles(xp_ref, o, values[at : at + lat_cols])
                at += lat_cols

    def sums(part):
        return take(
            lambda a, b: mix_ref[a:b].reshape((b - a) * lat_cols, hidden),
            part,
        )

    def mean(values):
        wide_mean = jnp.dot(values.astype(bf16), ones, preferred_element_type=f32)
        return jnp.concatenate([wide_mean] * (hidden // LANES), axis=1)

    def conv_inner(xp_ref, flip):
        def body(o, carry):
            conv_row(xp_ref, kb_ref, mix_ref, o, o, flip)
            return carry

        lax.fori_loop(REACH, lon_rows - REACH, body, 0)

    def conv_outer(xp_ref, flip):
        def body(k, carry):
            o = jnp.where(k < REACH, k, lon_rows - 2 * REACH + k)
            conv_row(xp_ref, kb_ref, mix_ref, o, o, flip)
            return carry

        lax.fori_loop(0, 2 * REACH, body, 0)

    def conv_own(xp_ref):
        for k in range(REACH):
            conv_row(xp_ref, kb_ref, mix_ref, k, k, True, range(REACH - k, TAPS))
            o = lon_rows - 1 - k
            conv_row(xp_ref, kb_ref, mix_ref, o, o, True, range(0, TAPS - REACH + k))

    def send_landing(at, xp_ref):
        for k in range(REACH):
            conv_row(xp_ref, kb_ref, land_ref, k - REACH, k, True, range(2 * REACH - k, TAPS))
            conv_row(xp_ref, kb_ref, land_ref, lon_rows + k, REACH + k, True, range(0, REACH - k))
        landed = land_ref[...].reshape(2 * strip, hidden).astype(bf16)
        g_state = lax.dot_general(landed, liftp_ref[...], ACROSS, preferred_element_type=f32)
        send(at, g_state[:strip], g_state[strip:])

    def forward(step, part, xp_ref, source_ref, target_ref, next_ref):
        mixed = sums(part)
        center = mixed - mean(mixed)
        inverse = lax.rsqrt(mean(center * center) + eps_norm)
        normal = center * inverse
        put(normal_ref, part, normal.astype(bf16), step)
        put(inverse_ref, part, inverse[:, :LANES], step)
        normed = (normal * gain_ref[...]).astype(bf16)
        total = take(
            lambda a, b: xp_ref[a + REACH : b + REACH, REACH : REACH + runs]
            .reshape((b - a) * lat_cols, hidden)
            .astype(f32),
            part,
        )
        piece = 256
        one = bf16(root_two_pi)
        three = bf16(root_two_pi * gelu_coef)
        half_one = bf16(0.5)
        for start in range(0, wide, piece):
            cut = slice(start, start + piece)
            z = jnp.dot(normed, up_ref[:, cut], preferred_element_type=f32).astype(bf16)
            square = z * z
            tanh_val = jnp.tanh(z * (one + three * square))
            share = half_one + half_one * tanh_val
            active = z * share
            rest = bf16(1.0) - share
            bend = z * (bf16(2.0) * one + bf16(6.0) * three * square)
            slope = share + share * (rest * bend)
            at = 0
            for a, b in part:
                size = (b - a) * lat_cols
                slope_ref[step, a * lat_cols : b * lat_cols, cut] = slope[at : at + size]
                at += size
            total = total + jnp.dot(active, down_ref[cut, :], preferred_element_type=f32)
        change = lax.dot_general(
            total.astype(bf16), outp_ref[...], ACROSS, preferred_element_type=f32
        )
        state = take(cells(source_ref), part) + change
        put(target_ref, part, state)
        if next_ref is not None:
            lifted = jnp.dot(state.astype(bf16), liftp_ref[...], preferred_element_type=f32)
            put_field(next_ref, part, lifted)

    def observe(moment, state_ref, target_ref):
        spots = lon_rows * runs
        by_point = lambda ref: jnp.concatenate([ref[moment, g] for g in range(tiles)], axis=1)
        cell = by_point(cell_ref)
        lane = lax.broadcasted_iota(jnp.int32, (points, slots), 1)
        first = ((lane // each) * TILE_LAT) % runs
        spot = (cell // TILE_LAT) * runs + first + cell % TILE_LAT
        weight = by_point(wts_ref)
        number = lax.broadcasted_iota(jnp.int32, (spots, slots), 0)
        lines = jnp.zeros((spots, slots), f32)
        for p in range(points):
            hit = spot[p : p + 1, :] == number
            lines = jnp.where(hit, lines + weight[p : p + 1, :], lines)
        op_ref[moment] = lines.T.astype(bf16)
        places = count * cap
        code = code_ref[moment]
        line = lax.broadcasted_iota(jnp.int32, (slots, LANES), 1).astype(f32)
        select = jnp.concatenate(
            [
                jnp.where(code - float(start) == line, 1.0, 0.0).astype(bf16)
                for start in range(0, places, LANES)
            ],
            axis=1,
        )
        data = late_in_ref[...].reshape(places, 2 * LANES)
        chosen = jnp.dot(select, data, preferred_element_type=f32)
        if moment == 0:
            data = early_in_ref[...].reshape(places, LANES)
            third = jnp.dot(select, data, preferred_element_type=f32)
            tiles3 = (chosen[:, :LANES], chosen[:, LANES:], third)
            back = [pltpu.roll(t, (LANES - n) % LANES, 1) for t, n in zip(tiles3, turns)]
            lane = lax.broadcasted_iota(jnp.int32, (slots, LANES), 1)
            start = channels - 2 * free
            weights = jnp.where(
                lane < start, back[2], jnp.where(lane < start + free, back[0], back[1])
            )
            weights = jnp.where(lane < channels, weights, 0.0)
            chosen = jnp.concatenate([third, weights], axis=1)
        chosen_ref[moment] = chosen
        size = slots // BLOCKS
        for block in range(BLOCKS):
            at = pl.ds(block, spots, stride=BLOCKS)
            mine = slice(block * size, (block + 1) * size)
            op = op_ref[moment, mine, :]
            equiv = jnp.dot(op, state_ref[at, :].astype(bf16), preferred_element_type=f32)
            chosen = chosen_ref[moment, mine, :]
            misfit = chosen[:, LANES:] * (equiv - chosen[:, :LANES])
            lane = lax.broadcasted_iota(jnp.int32, (size, LANES), 1)
            misfit = jnp.where(lane < channels, misfit, 0.0)
            target_ref[at, :] = lax.dot_general(
                op, misfit.astype(bf16), DOWN, preferred_element_type=f32
            )

    def gathered(part, at):
        g_lifted = (take(cells(gblk_ref), part).astype(f32) + sums(part)).astype(bf16)
        g_state = lax.dot_general(g_lifted, liftp_ref[...], ACROSS, preferred_element_type=f32)
        value = take(cells(cot_ref), part) + g_state
        if part != edges:
            return value
        return jnp.concatenate(
            [
                value[:strip] + halo_ref[at, 0].astype(f32),
                value[strip:-strip],
                value[-strip:] + halo_ref[at, 1].astype(f32),
            ],
            axis=0,
        )

    def backward(step, part, xp_ref, cotangent):
        g_block = jnp.dot(cotangent.astype(bf16), outp_ref[...], preferred_element_type=f32)
        g_block = g_block.astype(bf16)
        put(gblk_ref, part, g_block)
        piece = 256
        for start in range(0, wide, piece):
            cut = slice(start, start + piece)
            g_active = lax.dot_general(
                g_block, down_ref[cut, :], ACROSS, preferred_element_type=f32
            )
            slope = take(lambda a, b: slope_ref[step, a * lat_cols : b * lat_cols, cut], part)
            mid_ref[:, cut] = g_active.astype(bf16) * slope
        total = lax.dot_general(mid_ref[...], up_ref[...], ACROSS, preferred_element_type=f32)
        g_scaled = total * gain_ref[...]
        normal = take(leading(normal_ref, step), part).astype(f32)
        inverse = take(leading(inverse_ref, step), part)
        inverse = jnp.concatenate([inverse] * (hidden // LANES), axis=1)
        g_mixed = inverse * (g_scaled - mean(g_scaled) - normal * mean(g_scaled * normal))
        put_field(xp_ref, part, g_mixed)

    def leave(part):
        put(out_ref, part, gathered(part, 3))


    send_state(0)
    obs_start(1)
    conv_inner(xp0_ref, False)
    forward(0, inner, xp0_ref, one_ref, one_ref, xp1_ref)
    arrive_state(0, xp0_ref)
    conv_outer(xp0_ref, False)
    forward(0, edges, xp0_ref, one_ref, one_ref, xp1_ref)
    send_state(1)
    conv_inner(xp1_ref, False)
    forward(1, inner, xp1_ref, one_ref, two_ref, None)
    arrive_state(1, xp1_ref)
    obs_start(0)
    conv_outer(xp1_ref, False)
    forward(1, edges, xp1_ref, one_ref, two_ref, None)
    obs_wait(1)
    observe(1, two_ref, cot_ref)
    backward(1, edges, xp2_ref, take(cells(cot_ref), edges))
    send_landing(2, xp2_ref)
    backward(1, inner, xp2_ref, take(cells(cot_ref), inner))
    conv_own(xp2_ref)
    conv_inner(xp2_ref, True)
    obs_wait(0)
    observe(0, one_ref, pull_ref)
    arrive(2)

    def carried(part):
        value = gathered(part, 2) + take(cells(pull_ref), part)
        put(cot_ref, part, value)
        return value

    backward(0, edges, xp3_ref, carried(edges))
    send_landing(3, xp3_ref)
    backward(0, inner, xp3_ref, carried(inner))
    conv_own(xp3_ref)
    conv_inner(xp3_ref, True)
    leave(inner)
    arrive(3)
    leave(edges)


def turn_kernel(cells_hbm, out_ref, cells_ref, sem):
    lat_cols = out_ref.shape[1]
    lon_rows = cells_ref.shape[0] // lat_cols
    channels = out_ref.shape[0] // lon_rows
    runs = lat_cols // BLOCKS
    parts = sem.shape[0]
    size = lon_rows // parts
    loads = []
    for k in range(parts):
        at = pl.ds(k * size * lat_cols, size * lat_cols)
        load = pltpu.make_async_copy(cells_hbm.at[at], cells_ref.at[at], sem.at[k])
        load.start()
        loads.append(load)

    def body(o, carry):
        base = o * lat_cols
        rows = [cells_ref[pl.ds(base + k, runs, stride=BLOCKS), :] for k in range(BLOCKS)]
        turned = jnp.concatenate(rows, axis=0).T
        out_ref[pl.ds(o, channels, stride=lon_rows), :] = turned[:channels]
        return carry

    for k, load in enumerate(loads):
        load.wait()
        lax.fori_loop(k * size, (k + 1) * size, body, 0, unroll=2)


def shards(
    state_start,
    lift_weight,
    conv_kernel,
    norm_gain,
    up_weight,
    down_weight,
    out_weight,
    obs_cells,
    obs_weights,
    tile_counts,
    obs_owner,
    obs_values,
    obs_precision,
):
    channels, lon_rows, lat_cols = state_start.shape
    hidden, wide = up_weight.shape
    runs = lat_cols // BLOCKS
    count, cap = obs_values.shape[2:4]
    tiles, slot_total = obs_cells.shape[1:3]
    slots = tiles * slot_total
    amount = lon_rows * lat_cols

    vmem = pl.BlockSpec(memory_space=pltpu.VMEM)
    smem = pl.BlockSpec(memory_space=pltpu.SMEM)
    hbm = pl.BlockSpec(memory_space=pl.ANY)
    field = (lon_rows + 2 * REACH, runs + 2 * REACH, BLOCKS, hidden)
    result = pl.pallas_call(
        whole_kernel,
        out_shape=jax.ShapeDtypeStruct((amount, LANES), f32),
        in_specs=[vmem] * 4 + [hbm] * 2 + [vmem] * 3 + [smem, vmem] + [hbm] * 2,
        out_specs=vmem,
        scratch_shapes=[
            pltpu.VMEM((hidden, wide), bf16),
            pltpu.VMEM((wide, hidden), bf16),
            *[pltpu.VMEM((2, count, cap, channels), f32)] * 2,
            pltpu.VMEM((LANES, LANES), f32),
            pltpu.VMEM((LANES, LANES), f32),
            pltpu.VMEM((LANES, hidden), f32),
            pltpu.VMEM((LANES, hidden), bf16),
            pltpu.VMEM((LANES, hidden), bf16),
            pltpu.VMEM((TAPS * TAPS, BLOCKS, hidden), bf16),
            *[pltpu.VMEM(field, bf16)] * 4,
            *[pltpu.VMEM((amount, LANES), f32)] * 4,
            pltpu.VMEM((lon_rows, runs, BLOCKS, hidden), f32),
            pltpu.VMEM((2, amount, hidden), bf16),
            pltpu.VMEM((2, amount, LANES), f32),
            pltpu.VMEM((2, amount, wide), bf16),
            pltpu.VMEM((amount, hidden), bf16),
            pltpu.VMEM((amount // 2, wide), bf16),
            pltpu.VMEM((2 * REACH, runs, BLOCKS, hidden), f32),
            pltpu.VMEM((4, 2, REACH * lat_cols, LANES), bf16),
            pltpu.VMEM((4, 2, REACH * lat_cols, LANES), bf16),
            pltpu.VMEM((2, slots, LANES), f32),
            pltpu.VMEM((2, slots, lon_rows * runs), bf16),
            pltpu.VMEM((2, slots, 2 * LANES), f32),
            *[
                pltpu.VMEM((count, cap, 2 * LANES), bf16),
                pltpu.VMEM((count, cap, LANES), bf16),
            ]
            * 2,
            pltpu.SemaphoreType.DMA((8,)),
            pltpu.SemaphoreType.DMA((8,)),
            pltpu.SemaphoreType.DMA((2, count - 1)),
            pltpu.SemaphoreType.DMA((2, count - 1)),
            pltpu.SemaphoreType.DMA((2,)),
            pltpu.SemaphoreType.DMA((4,)),
        ],
        compiler_params=pltpu.CompilerParams(
            vmem_limit_bytes=VMEM_LIMIT, collective_id=0, has_side_effects=True
        ),
    )(
        state_start.reshape(channels * lon_rows, lat_cols),
        lift_weight,
        conv_kernel,
        norm_gain.reshape(1, hidden),
        up_weight,
        down_weight,
        out_weight.T,
        obs_cells.transpose(0, 1, 3, 2),
        obs_weights.transpose(0, 1, 3, 2),
        tile_counts,
        obs_owner.transpose(0, 2, 1),
        obs_values[:, 0],
        obs_precision[:, 0],
    )
    turned = pl.pallas_call(
        turn_kernel,
        out_shape=jax.ShapeDtypeStruct((channels * lon_rows, lat_cols), f32),
        in_specs=[hbm],
        out_specs=vmem,
        scratch_shapes=[pltpu.VMEM((amount, LANES), f32), pltpu.SemaphoreType.DMA((4,))],
        compiler_params=pltpu.CompilerParams(vmem_limit_bytes=VMEM_LIMIT),
    )(result)
    return turned.reshape(channels, lon_rows, lat_cols)


def solution(mesh):
    placed = (
        P("member", "lon", None),
        P(),
        P(),
        P(),
        P(),
        P(),
        P(),
        P("member", "lon", None, None),
        P("member", "lon", None, None),
        P("member", "lon"),
        P("member", "lon", None),
        P("member", "lon", None, None, None),
        P("member", "lon", None, None, None),
    )
    return jax.shard_map(
        shards, mesh=mesh, in_specs=placed, out_specs=P("member", "lon", None), check_vma=False
    )
```
